32 devices in a mesh: tower: 2 (over y), batch: 16 (over z, x, core).
Axes of the slice: x: 2, y: 2, z: 4, core: 2. Of those that a mesh axis runs over, the one named last changes fastest.
Arguments:
- img_feat: bfloat16 [3072, 1536], P('batch'), may hold values from -6 to 6
- txt_feat: bfloat16 [3072, 1152], P('batch'), may hold values from -6 to 6
- img_proj: bfloat16 [1536, 1152], P('batch', 'tower'), may hold values from -0.15625 to 0.15625
- txt_proj: bfloat16 [1152, 1152], P('batch', 'tower'), may hold values from -0.1875 to 0.1875
- valid_rows: int32 [16], P('batch'), may hold values from 1 to 192, 2304 in all
Outputs:
- img_grad: bfloat16 [3072, 1536], P('batch', 'tower')
- txt_grad: bfloat16 [3072, 1152], P('batch', 'tower')
- img_proj_grad: float32 [1536, 1152], P('batch', 'tower')
- txt_proj_grad: float32 [1152, 1152], P('batch', 'tower')
The draws below stay inside these ranges and needn't reach their ends.
Inputs may be any that keep to these rules, and one draw needn't show every extreme that they name: valid_rows[c] counts the valid leading rows of batch shard c; the entries sum to 2304.
All inputs are finite; a program needn't handle non-finite values.
Results may differ from the reference program's by a relative error of at most 0.0064.
Values may be sent and summed in bfloat16 or wider, within the bound.
No kernel may reach another device: no remote copies, remote signals or barrier semaphores. Data moves between devices by JAX's collectives and lax.ppermute only.
A program may use at most 128 MiB of HBM per device.

```python
import math
import jax
import jax.numpy as jnp
import numpy as np
from jax import lax

DI = 1536
DT = 1152
E = 1152
TOK_DEV = 192
B = 3072
VALID = 2304
N_BATCH = 16


def strengthened(array, rng, source, target, parts, factor):
    owner, partner = [(jnp.arange(array.shape[position]) // (array.shape[position] // parts)).reshape([-1 if axis == position else 1 for axis in range(array.ndim)]) for position in (source, target)]
    chosen = jax.random.permutation(rng, parts)[partner]
    strong = (owner == chosen) | (owner == (partner + parts // 2) % parts)
    return jnp.where(strong, factor * array, array)


def block_scale(stream_key, shape, pieces, low, high):
    level = 1.0
    for axis_at, blocks in pieces:
        heights = jax.random.uniform(jax.random.fold_in(jax.random.fold_in(stream_key, 6), axis_at), (blocks,), jnp.float32, low / len(pieces), high / len(pieces))
        level = level * jnp.repeat(jnp.exp(heights), shape[axis_at] // blocks).reshape((-1,) + (1,) * (len(shape) - 1 - axis_at))
    return level


def length_profile(number_of, total, limit, slope):
    portions = [(1 << 20) // math.isqrt(standing ** slope) + 1 for standing in range(2, number_of + 1)]
    surplus, given = total - limit - (number_of - 1), [1] * (number_of - 1)
    while surplus > 0:
        movable = [i for i in range(number_of - 1) if given[i] < limit]
        pool, remaining = sum([portions[i] for i in movable]), surplus
        for i in movable:
            more = min(limit - given[i], max(1, remaining * portions[i] // pool), surplus)
            given[i] = given[i] + more
            surplus = surplus - more
    return np.array([limit] + given)


def ragged_sizes(rng, count, total, bound, slope):
    if count == 2:
        one = jax.random.randint(rng, (), max(1, total - bound), min(bound, total - 1) + 1)
        return jnp.stack([one, total - one])
    lengths = jnp.asarray(length_profile(count, total, bound, slope), jnp.int32)
    pairs = (count - 1) // 2
    donor, receiver = lengths[1:1 + 2 * pairs:2], lengths[2:2 + 2 * pairs:2]
    room = jnp.minimum(donor - 1, bound - receiver)
    moved = jax.random.randint(jax.random.fold_in(rng, 1), (pairs,), 0, 1 << 20) % (room + 1)
    lengths = lengths.at[1:1 + 2 * pairs:2].set(donor - moved).at[2:2 + 2 * pairs:2].set(receiver + moved)
    return lengths[jax.random.permutation(jax.random.fold_in(rng, 2), count)]


def bell_draw(rng, extent, spread, limit, split=(), held_as=jnp.bfloat16):
    gain = block_scale(rng, extent, split, -0.22, 0.18) if split else 1.0
    result = jax.random.normal(rng, extent, jnp.float32) * spread * gain
    return jnp.minimum(jnp.maximum(result, -limit), limit).astype(held_as)


def gaussian_with(key, extent, scale, bound, shards, heavy, kind=jnp.bfloat16):
    array = scale * jax.random.normal(key, extent, jnp.float32)
    if shards:
        array = array * block_scale(key, extent, shards, -0.22, 0.18)
    return jnp.clip(strengthened(array, jax.random.fold_in(key, 3), *heavy), -bound, bound).astype(kind)


def setup_inputs(seed: int = 0) -> dict:
    arg_keys = jax.random.split(jax.random.key(seed), 6)
    return {
        "img_feat": gaussian_with(arg_keys[0], (B, DI), 1.0, 6.0, ((0, 16),), (0, 1, 16, 2.0)),
        "txt_feat": gaussian_with(arg_keys[1], (B, DT), 1.0, 6.0, ((0, 16),), (0, 1, 16, 2.0)),
        "img_proj": bell_draw(arg_keys[2], (DI, E), DI ** -0.5, 0.15625, ((0, 16), (1, 2))),
        "txt_proj": bell_draw(arg_keys[3], (DT, E), DT ** -0.5, 0.1875, ((0, 16), (1, 2))),
        "valid_rows": ragged_sizes(arg_keys[4], N_BATCH, VALID, TOK_DEV, 2).astype(jnp.int32),
    }


similarity_sharpness = 10.0
similarity_shift = -4.0
objective_multiplier = 262144.0
epsilon = 1e-06

def normalize(proj_rows):
    norms = jnp.sqrt(lax.optimization_barrier(jnp.sum(proj_rows * proj_rows, axis=1)) + epsilon)
    return ((proj_rows / norms[:, None]).astype(jnp.bfloat16), norms)

def side_grad(local_embedding, foreign_feature_vector, row_mask, matched_tally):
    total_rows = local_embedding.shape[0]
    blocks = local_embedding.reshape(total_rows // TOK_DEV, TOK_DEV, local_embedding.shape[1])
    block_ids = jnp.arange(total_rows // TOK_DEV, dtype=jnp.int32)
    other_ids = jnp.arange(total_rows, dtype=jnp.int32)

    def one_block(item):
        tile_portion, block_id = item
        first_row = block_id * TOK_DEV
        mine_ids = first_row + jnp.arange(TOK_DEV, dtype=jnp.int32)
        block_mask = lax.dynamic_slice_in_dim(row_mask, first_row, TOK_DEV, 0)
        similarity_matrix = similarity_sharpness * jnp.dot(tile_portion, foreign_feature_vector.T, preferred_element_type=jnp.float32) + similarity_shift
        signs = jnp.where(mine_ids[:, None] == other_ids[None, :], 1.0, -1.0).astype(jnp.float32)
        pair_grad = -signs * jax.nn.sigmoid(-signs * similarity_matrix) * block_mask[:, None] * row_mask[None, :]
        return jnp.dot(pair_grad.astype(jnp.bfloat16), foreign_feature_vector, preferred_element_type=jnp.float32)
    accumulated_aggregate = lax.map(one_block, (blocks, block_ids)).reshape(total_rows, foreign_feature_vector.shape[1])
    return accumulated_aggregate * (similarity_sharpness * objective_multiplier / matched_tally)

def back_norm(embed, grad_embed, norms):
    embed_f = embed.astype(jnp.float32)
    along = lax.optimization_barrier(jnp.sum(embed_f * grad_embed, axis=1, keepdims=True))
    return ((grad_embed - embed_f * along) / norms[:, None]).astype(jnp.bfloat16)

def reference(img_feat, txt_feat, img_proj, txt_proj, valid_rows):
    p_img = jnp.dot(img_feat, img_proj, preferred_element_type=jnp.float32)
    p_txt = jnp.dot(txt_feat, txt_proj, preferred_element_type=jnp.float32)
    u_emb, n_img = normalize(p_img)
    v_emb, n_txt = normalize(p_txt)
    local_ids = jnp.arange(TOK_DEV, dtype=jnp.int32)
    row_mask = (local_ids[None, :] < valid_rows[:, None]).astype(jnp.float32).reshape(-1)
    matched_tally = jnp.sum(valid_rows).astype(jnp.float32)
    grad_u = side_grad(u_emb, v_emb, row_mask, matched_tally)
    grad_v = side_grad(v_emb, u_emb, row_mask, matched_tally)
    dp_img = back_norm(u_emb, grad_u, n_img)
    dp_txt = back_norm(v_emb, grad_v, n_txt)
    img_grad = jnp.dot(dp_img, img_proj.T, preferred_element_type=jnp.float32).astype(jnp.bfloat16)
    txt_grad = jnp.dot(dp_txt, txt_proj.T, preferred_element_type=jnp.float32).astype(jnp.bfloat16)
    img_proj_grad = jnp.dot(img_feat.T, dp_img, preferred_element_type=jnp.float32)
    txt_proj_grad = jnp.dot(txt_feat.T, dp_txt, preferred_element_type=jnp.float32)
    return (img_grad, txt_grad, img_proj_grad, txt_proj_grad)
```

```python
import jax
import jax.numpy as jnp
from jax import lax
from jax.sharding import PartitionSpec as P

sharpness = 10.0
shift = -4.0
multiplier = 262144.0
epsilon = 1e-06

F32, BF16 = jnp.float32, jnp.bfloat16


def dot(a, b, dims):
    return lax.dot_general(a, b, (dims, ((), ())), preferred_element_type=F32)


class Ring:
    def __init__(self, batch_size):
        n = self.n = batch_size // 2
        half = n // 2
        self.order = [2 * r if r < half else 2 * (n - 1 - r) + 1 for r in range(n)]
        place = {chip: r for r, chip in enumerate(self.order)}
        self.place = [place[chip] for chip in range(n)]
        self.fwd = self._perm(1)
        self.bwd = self._perm(-1)
        self.core = [(b, b ^ 1) for b in range(batch_size)]
        chip = lax.axis_index("batch") // 2
        self.pos = jnp.where(chip % 2 == 0, chip // 2, n - 1 - chip // 2)

    def _perm(self, step):
        pairs = []
        for r, chip in enumerate(self.order):
            to = self.order[(r + step) % self.n]
            pairs += [(2 * chip + c, 2 * to + c) for c in range(2)]
        return pairs

    def right(self, x):
        return lax.ppermute(x, "batch", self.fwd)

    def left(self, x):
        return lax.ppermute(x, "batch", self.bwd)

    def other_core(self, x):
        return lax.ppermute(x, "batch", self.core)

    def relative(self, stack):
        by_place = jnp.stack([stack[chip] for chip in self.order])
        twice = jnp.concatenate([by_place, by_place])
        return lax.dynamic_slice_in_dim(twice, self.pos, self.n, 0)

    def absolute(self, stack):
        twice = jnp.concatenate([stack, stack])
        by_place = lax.dynamic_slice_in_dim(twice, self.n - self.pos, self.n, 0)
        return jnp.stack([by_place[r] for r in self.place])

    def gather_steps(self, x, cut):
        n = self.n
        f = b = x
        for k in range(1, n // 2):
            f, b = self.right(f), self.left(b)
            yield [(n - k, f), (k, b)]
        f, b = self.right(f[:cut]), self.left(b[cut:])
        yield [(n // 2, jnp.concatenate([f, b]))]


def swap(x):
    return lax.ppermute(x, "tower", [(0, 1), (1, 0)])


def shards(img_feat, txt_feat, img_proj, txt_proj, valid_rows):
    nb = lax.axis_size("batch")
    ring = Ring(nb)
    n = ring.n
    tower = lax.axis_index("tower")
    is_image = tower == 0
    core = lax.axis_index("batch") % 2
    rows = img_feat.shape[0]
    ri, half = img_proj.shape
    rt = txt_proj.shape[0]

    count_rows = jnp.broadcast_to(valid_rows.astype(BF16)[:, None], (8, half))
    w = jnp.concatenate([img_proj, txt_proj, count_rows])
    got = {0: w}
    for step in ring.gather_steps(w, ri):
        got.update(step)

    def columns(feat, width):
        t = feat.T.reshape(n, 2, width, rows)
        keep = lax.dynamic_index_in_dim(t, core, 1, keepdims=False)
        give = lax.dynamic_index_in_dim(t, 1 - core, 1, keepdims=False)
        return ring.relative(jnp.concatenate([keep, ring.other_core(give)], axis=2))

    img_t = columns(img_feat, ri).reshape(n * ri, 2 * rows)
    txt_t = columns(txt_feat, rt).reshape(n * rt, 2 * rows)

    w_img = jnp.stack([got[d][:ri] for d in range(n)])
    w_txt = jnp.stack([got[d][ri : ri + rt] for d in range(n)])
    count = sum(got[d][ri + rt, 0].astype(F32) for d in range(n))
    count = jnp.broadcast_to(count, (8, 128))
    count = (count + ring.other_core(count))[0, 0]

    p_img2 = dot(img_t, w_img.reshape(n * ri, half), ((0,), (0,)))
    p_txt2 = dot(txt_t, w_txt.reshape(n * rt, half), ((0,), (0,)))
    p_give = jnp.concatenate([p_img2[rows:], p_txt2[rows:]], axis=0)
    p_got = ring.other_core(p_give)
    p_img = p_img2[:rows] + p_got[:rows]
    p_txt = p_txt2[:rows] + p_got[rows:]

    sq = jnp.stack([jnp.sum(p_img * p_img, axis=1), jnp.sum(p_txt * p_txt, axis=1)])
    sq = sq + swap(sq)
    norms = jnp.sqrt(sq + epsilon)
    n_img, n_txt = norms[0], norms[1]
    mask = jnp.arange(rows, dtype=jnp.int32) < valid_rows[0]
    u = jnp.where(mask[:, None], p_img / n_img[:, None], 0.0).astype(BF16)
    v = jnp.where(mask[:, None], p_txt / n_txt[:, None], 0.0).astype(BF16)
    mine_norm = jnp.where(is_image, n_img, n_txt)

    mine_o = jnp.where(is_image, u, v)
    other_o = jnp.where(is_image, v, u)
    other_x = swap(mine_o)
    mine_x = swap(other_o)
    own = jnp.concatenate([mine_o, mine_x], axis=1)
    own2 = jnp.concatenate([own, ring.other_core(own)], axis=0)
    own2_o, own2_x = own2[:, :half], own2[:, half:]

    def logits(fo, fx):
        s = dot(own2_o, fo, ((1,), (1,))) + dot(own2_x, fx, ((1,), (1,)))
        return sharpness * s + shift

    s = logits(other_o, other_x)
    diag = (
        lax.broadcasted_iota(jnp.int32, s.shape, 0) == lax.broadcasted_iota(jnp.int32, s.shape, 1)
    )
    g = jax.nn.sigmoid(jnp.where(diag, -s, s))
    qb = jnp.where(diag, -g, g).astype(BF16)
    acc_o = dot(qb, other_o, ((1,), (0,)))
    acc_x = dot(qb, other_x, ((1,), (0,)))
    cut = rows // 2
    for so, sx in zip(ring.gather_steps(other_o, cut), ring.gather_steps(other_x, cut)):
        fo = jnp.concatenate([c for _, c in so])
        fx = jnp.concatenate([c for _, c in sx])
        qb = jax.nn.sigmoid(logits(fo, fx)).astype(BF16)
        acc_o = acc_o + dot(qb, fo, ((1,), (0,)))
        acc_x = acc_x + dot(qb, fx, ((1,), (0,)))
    acc = jnp.concatenate([acc_o, acc_x], axis=1)
    acc = acc[:rows] + ring.other_core(acc[rows:])

    du = acc * (sharpness * multiplier / count)
    mine_f = own.astype(F32)
    along = jnp.sum(mine_f * du, axis=1, keepdims=True)
    dp = jnp.where(mask[:, None], (du - mine_f * along) / mine_norm[:, None], 0.0).astype(BF16)
    dp_mine, dp_give = dp[:, :half], dp[:, half:]
    dp_got = swap(dp_give)
    dp_img = jnp.where(is_image, dp_mine, dp_got)
    dp_txt = jnp.where(is_image, dp_got, dp_mine)
    dp_both = jnp.concatenate([dp_img, dp_txt], axis=1)
    dp2 = jnp.concatenate([dp_both, ring.other_core(dp_both)], axis=0)

    g_img = dot(img_t, dp2[:, :half], ((1,), (0,))).reshape(n, ri, half)
    g_txt = dot(txt_t, dp2[:, half:], ((1,), (0,))).reshape(n, rt, half)

    def part(d):
        return jnp.concatenate([g_img[d], g_txt[d]])

    h = n // 2
    f = ring.right(g_img[h].astype(BF16))
    b = ring.left(g_txt[h].astype(BF16))
    for k in range(h - 1, 0, -1):
        pf, pb = part(k), part(n - k)
        if k == h - 1:
            f = jnp.concatenate([g_img[k] + f.astype(F32), g_txt[k]])
            b = jnp.concatenate([g_img[n - k], g_txt[n - k] + b.astype(F32)])
        else:
            f, b = pf + f.astype(F32), pb + b.astype(F32)
        f, b = ring.right(f.astype(BF16)), ring.left(b.astype(BF16))
    total = part(0) + f.astype(F32) + b.astype(F32)

    w_all = jnp.concatenate([w_img.reshape(n * ri, half), w_txt.reshape(n * rt, half)])
    w_sib = ring.other_core(w_all)

    def weights(at, width):
        a = ring.absolute(w_all[at : at + n * width].reshape(n, width, half))
        s = ring.absolute(w_sib[at : at + n * width].reshape(n, width, half))
        both = jnp.stack([jnp.where(core == 0, a, s), jnp.where(core == 0, s, a)], axis=1)
        return both.reshape(2 * n * width, half)

    wi, wt = weights(0, ri), weights(n * ri, rt)

    def halves(wm):
        m = wm.shape[0] // 2
        keep = lax.dynamic_slice_in_dim(wm, tower * m, m, 0)
        give = lax.dynamic_slice_in_dim(wm, (1 - tower) * m, m, 0)
        return keep, give

    (ki, gi), (kt, gt) = halves(wi), halves(wt)
    give = jnp.concatenate(
        [
            dot(dp_img, gi, ((1,), (1,))).astype(BF16),
            dot(dp_txt, gt, ((1,), (1,))).astype(BF16),
        ],
        axis=1,
    )
    recv = swap(give).astype(F32)
    mi = ki.shape[0]
    img_grad = dot(dp_img, ki, ((1,), (1,))) + recv[:, :mi]
    txt_grad = dot(dp_txt, kt, ((1,), (1,))) + recv[:, mi:]
    return (img_grad.astype(BF16), txt_grad.astype(BF16), total[:ri], total[ri:])


def solution(mesh):
    in_specs = (
        P("batch", None),
        P("batch", None),
        P("batch", "tower"),
        P("batch", "tower"),
        P("batch"),
    )
    out_specs = (P("batch", "tower"),) * 4
    return jax.shard_map(shards, mesh=mesh, in_specs=in_specs, out_specs=out_specs, check_vma=False)
```

```python
import functools

import jax
import jax.numpy as jnp
from jax import lax
from jax.experimental import pallas as pl
from jax.experimental.pallas import tpu as pltpu
from jax.sharding import PartitionSpec as P

sharpness = 10.0
shift = -4.0
multiplier = 262144.0
epsilon = 1e-06

F32, BF16 = jnp.float32, jnp.bfloat16


def dot(a, b, dims):
    return lax.dot_general(a, b, (dims, ((), ())), preferred_element_type=F32)


def nt(a, b):
    return dot(a, b, ((1,), (1,)))


def nn(a, b):
    return dot(a, b, ((1,), (0,)))


def up16(k):
    return -(-k // 16) * 16


def call(body, outs, scalars, arrays, alias=None):
    smem = pl.BlockSpec(memory_space=pltpu.SMEM)
    vmem = pl.BlockSpec(memory_space=pltpu.VMEM)
    return pl.pallas_call(
        body,
        out_shape=[jax.ShapeDtypeStruct(s, t) for s, t in outs],
        in_specs=[smem] * len(scalars) + [vmem] * len(arrays),
        out_specs=[vmem] * len(outs),
        input_output_aliases=alias or {},
        compiler_params=pltpu.CompilerParams(vmem_limit_bytes=48 * 1024 * 1024),
    )(*scalars, *arrays)


class Ring:
    def __init__(self, batch_size):
        n = self.n = batch_size // 2
        half = n // 2
        self.order = [2 * r if r < half else 2 * (n - 1 - r) + 1 for r in range(n)]
        self.fwd = self._perm(1)
        self.bwd = self._perm(-1)
        self.core = [(b, b ^ 1) for b in range(batch_size)]
        chip = lax.axis_index("batch") // 2
        self.pos = jnp.where(chip % 2 == 0, chip // 2, n - 1 - chip // 2)
        place = (self.pos + jnp.arange(n, dtype=jnp.int32)) % n
        self.chips = jnp.where(place < half, 2 * place, 2 * (n - 1 - place) + 1).astype(jnp.int32)

    def _perm(self, step):
        pairs = []
        for r, chip in enumerate(self.order):
            to = self.order[(r + step) % self.n]
            pairs += [(2 * chip + c, 2 * to + c) for c in range(2)]
        return pairs

    def right(self, x):
        return lax.ppermute(x, "batch", self.fwd)

    def left(self, x):
        return lax.ppermute(x, "batch", self.bwd)

    def other_core(self, x):
        return lax.ppermute(x, "batch", self.core)

    def gather(self, x, cut):
        f = b = x
        for _ in range(1, self.n // 2):
            f, b = self.right(f), self.left(b)
            yield f, b
        yield self.right(f[:cut]), self.left(b[cut:])


def swap(x):
    return lax.ppermute(x, "tower", [(0, 1), (1, 0)])


def project(n, rpi, rpt, half, slot_ref, img_ref, txt_ref, *refs):
    chunks, (wi_ref, wt_ref, pi_ref, pt_ref, sq_ref) = refs[:-5], refs[-5:]
    it = iter(chunks)
    h = n // 2
    for sibling in range(2):
        for d in range(n):
            b = slot_ref[sibling, d]
            if d == h:
                wi_ref[b] = next(it)[...]
                wt_ref[b] = next(it)[...]
            else:
                c = next(it)
                wi_ref[b] = c[:rpi]
                wt_ref[b] = c[rpi:]
    pi = nn(img_ref[...], wi_ref[...].reshape(2 * n * rpi, half))
    pt = nn(txt_ref[...], wt_ref[...].reshape(2 * n * rpt, half))
    pi_ref[...] = pi
    pt_ref[...] = pt
    si = jnp.sum(pi * pi, axis=1, keepdims=True)
    st = jnp.sum(pt * pt, axis=1, keepdims=True)
    lane = lax.broadcasted_iota(jnp.int32, (pi.shape[0], 128), 1)
    sq_ref[...] = jnp.where(lane == 0, si, st).T[:8]


def normalize(s_ref, pi_ref, pt_ref, sq_ref, got_ref, mine_ref, other_ref, norm_ref):
    tower, valid = s_ref[0], s_ref[1]
    rows = pi_ref.shape[0]
    sq = sq_ref[...] + got_ref[...]
    norm = jnp.sqrt(sq + epsilon).T
    ni, nt_ = norm[:, 0:1], norm[:, 1:2]
    keep = lax.broadcasted_iota(jnp.int32, (rows, 1), 0) < valid
    u = jnp.where(keep, pi_ref[...] / ni, 0.0)
    v = jnp.where(keep, pt_ref[...] / nt_, 0.0)
    image = tower == 0
    mine_ref[...] = jnp.where(image, u, v).astype(BF16)
    other_ref[...] = jnp.where(image, v, u).astype(BF16)
    norm_ref[...] = jnp.where(image, ni, nt_)


def pairs(chunks, first, *refs):
    half = refs[0].shape[1]
    mine, refs = refs[:4], refs[4:]
    fs, refs = refs[: 2 * chunks], refs[2 * chunks :]
    fo = jnp.concatenate([f[...] for f in fs[:chunks]]) if chunks > 1 else fs[0][...]
    fx = jnp.concatenate([f[...] for f in fs[chunks:]]) if chunks > 1 else fs[1][...]
    ins, outs = (None, refs) if first else (refs[:2], refs[2:])
    for side in range(2):
        mo, mx = mine[2 * side], mine[2 * side + 1]
        s = sharpness * (nt(mo[...], fo) + nt(mx[...], fx)) + shift
        if first and side == 0:
            r = lax.broadcasted_iota(jnp.int32, s.shape, 0)
            c = lax.broadcasted_iota(jnp.int32, s.shape, 1)
            g = jax.nn.sigmoid(jnp.where(r == c, -s, s))
            g = jnp.where(r == c, -g, g)
        else:
            g = jax.nn.sigmoid(s)
        qb = g.astype(BF16)
        for at, f in ((0, fo), (half, fx)):
            part = nn(qb, f)
            cols = slice(at, at + half)
            outs[side][:, cols] = part if first else ins[side][:, cols] + part


def back_norm(s_ref, c_ref, acc_ref, got_ref, mo_ref, mx_ref, norm_ref, do_ref, dx_ref):
    valid, coef = s_ref[1], c_ref[0]
    rows, half = mo_ref.shape
    du = (acc_ref[...] + got_ref[...]) * coef
    duo, dux = du[:, :half], du[:, half:]
    mo, mx = mo_ref[...].astype(F32), mx_ref[...].astype(F32)
    along = jnp.sum(mo * duo, axis=1, keepdims=True) + jnp.sum(mx * dux, axis=1, keepdims=True)
    keep = lax.broadcasted_iota(jnp.int32, (rows, 1), 0) < valid
    norm = norm_ref[...]
    do_ref[...] = jnp.where(keep, (duo - mo * along) / norm, 0.0).astype(BF16)
    dx_ref[...] = jnp.where(keep, (dux - mx * along) / norm, 0.0).astype(BF16)


def products(n, first, s_ref, chip_ref, do_ref, dg_ref, so_ref, sg_ref, ai, bi, at, bt, *outs):
    image = s_ref[0] == 0
    do, dg, so, sg = do_ref[...], dg_ref[...], so_ref[...], sg_ref[...]
    img, img_s = jnp.where(image, do, dg), jnp.where(image, so, sg)
    txt, txt_s = jnp.where(image, dg, do), jnp.where(image, sg, so)
    rpi = ai.shape[1]
    h = n // 2
    for d in [h] if first else [d for d in range(n) if d != h]:
        q = chip_ref[d]
        gi = nn(ai[q], img) + nn(bi[q], img_s)
        gt = nn(at[q], txt) + nn(bt[q], txt_s)
        if first:
            outs[0][...] = gi.astype(BF16)
            outs[1][...] = gt.astype(BF16)
        else:
            outs[0][d, :rpi] = gi
            outs[0][d, rpi:] = gt


def shards(img_feat, txt_feat, img_proj, txt_proj, valid_rows):
    nb = lax.axis_size("batch")
    ring = Ring(nb)
    n, h = ring.n, ring.n // 2
    tower = lax.axis_index("tower")
    core = lax.axis_index("batch") % 2
    rows = img_feat.shape[0]
    ri, half = img_proj.shape
    rt = txt_proj.shape[0]
    rpi, rpt = up16(ri), up16(rt + 1)
    flags = jnp.stack([tower.astype(jnp.int32), valid_rows[0]])

    count_rows = jnp.broadcast_to(valid_rows.astype(BF16)[:, None], (rpt - rt, half))
    pad = jnp.zeros((rpi - ri, half), BF16)
    w = jnp.concatenate([img_proj] + [pad] * (rpi > ri) + [txt_proj, count_rows])
    at = {0: w}
    sib = {0: ring.other_core(w)}
    for k, (f, b) in enumerate(ring.gather(w, rpi), 1):
        if k < h:
            at[n - k], at[k] = f, b
            sib[n - k], sib[k] = ring.other_core(f), ring.other_core(b)
        else:
            at[h], sib[h] = (f, b), (ring.other_core(f), ring.other_core(b))

    def flat(chunks):
        out = []
        for d in range(n):
            out += list(chunks[d]) if d == h else [chunks[d]]
        return out

    def spread(feat, r, rp):
        if rp == r:
            return feat
        f = feat.reshape(rows, nb, r)
        return jnp.pad(f, ((0, 0), (0, 0), (0, rp - r))).reshape(rows, nb * rp)

    slots = jnp.stack([2 * ring.chips + core, 2 * ring.chips + 1 - core]).astype(jnp.int32)
    wi, wt, p_img, p_txt, sq = call(
        functools.partial(project, n, rpi, rpt, half),
        [
            ((nb, rpi, half), BF16),
            ((nb, rpt, half), BF16),
            ((rows, half), F32),
            ((rows, half), F32),
            ((8, rows), F32),
        ],
        [slots],
        [spread(img_feat, ri, rpi), spread(txt_feat, rt, rpt)] + flat(at) + flat(sib),
    )
    mine_o, other_o, norm = call(
        normalize,
        [((rows, half), BF16), ((rows, half), BF16), ((rows, 1), F32)],
        [flags],
        [p_img, p_txt, sq, swap(sq)],
    )

    other_x = swap(mine_o)
    mine_x = swap(other_o)
    mine = [mine_o, mine_x, ring.other_core(mine_o), ring.other_core(mine_x)]
    acc_type = [((rows, 2 * half), F32)] * 2
    acc = call(functools.partial(pairs, 1, True), acc_type, [], mine + [other_o, other_x])
    cut = rows // 2
    for so, sx in zip(ring.gather(other_o, cut), ring.gather(other_x, cut)):
        acc = call(
            functools.partial(pairs, 2, False),
            acc_type,
            [],
            mine + list(so) + list(sx) + list(acc),
            {8: 0, 9: 1},
        )
    count = jnp.sum(wt[:, rt, 0].astype(F32))
    coef = (sharpness * multiplier / count).reshape(1)
    dp_o, dp_x = call(
        back_norm,
        [((rows, half), BF16)] * 2,
        [flags, coef],
        [acc[0], ring.other_core(acc[1]), mine_o, mine_x, norm],
    )
    dp_got = swap(dp_x)
    dps = [dp_o, dp_got, ring.other_core(dp_o), ring.other_core(dp_got)]

    def columns(feat, r, rp):
        t = feat.T.reshape(n, 2, r, rows)
        t = jnp.pad(t, ((0, 0), (0, 0), (0, rp - r), (0, 0)))
        keep = lax.dynamic_index_in_dim(t, core, 1, keepdims=False)
        give = lax.dynamic_index_in_dim(t, 1 - core, 1, keepdims=False)
        return [keep, ring.other_core(give)]

    feats = columns(img_feat, ri, rpi) + columns(txt_feat, rt, rpt)

    def product(first, outs, ds):
        return call(functools.partial(products, n, first), outs, [flags, ring.chips], ds + feats)

    f, b = product(True, [((rpi, half), BF16), ((rpt, half), BF16)], dps)
    dp_o, dp_got, f, b = lax.optimization_barrier((dp_o, dp_got, f, b))
    (g,) = product(False, [((n, rpi + rpt, half), F32)], [dp_o, dp_got] + dps[2:])
    f, b = ring.right(f), ring.left(b)
    for k in range(h - 1, 0, -1):
        pf, pb = g[k], g[n - k]
        if k == h - 1:
            f = jnp.concatenate([pf[:rpi] + f.astype(F32), pf[rpi:]])
            b = jnp.concatenate([pb[:rpi], pb[rpi:] + b.astype(F32)])
        else:
            f, b = pf + f.astype(F32), pb + b.astype(F32)
        f, b = ring.right(f.astype(BF16)), ring.left(b.astype(BF16))
    total = g[0] + f.astype(F32) + b.astype(F32)

    is_image = tower == 0
    dp_img = jnp.where(is_image, dp_o, dp_got)
    dp_txt = jnp.where(is_image, dp_got, dp_o)

    def halves(wm, r):
        wm = wm[:, :r].reshape(nb * r, half)
        m = nb * r // 2
        keep = lax.dynamic_slice_in_dim(wm, tower * m, m, 0)
        give = lax.dynamic_slice_in_dim(wm, (1 - tower) * m, m, 0)
        return keep, give

    (ki, gi), (kt, gt) = halves(wi, ri), halves(wt, rt)
    img_got = swap(nt(dp_img, gi).astype(BF16)).astype(F32)
    txt_got = swap(nt(dp_txt, gt).astype(BF16)).astype(F32)
    img_grad = nt(dp_img, ki) + img_got
    txt_grad = nt(dp_txt, kt) + txt_got
    return (img_grad.astype(BF16), txt_grad.astype(BF16), total[:ri], total[rpi : rpi + rt])


def solution(mesh):
    in_specs = (
        P("batch", None),
        P("batch", None),
        P("batch", "tower"),
        P("batch", "tower"),
        P("batch"),
    )
    out_specs = (P("batch", "tower"),) * 4
    return jax.shard_map(shards, mesh=mesh, in_specs=in_specs, out_specs=out_specs, check_vma=False)
```

```python
import functools

import jax
import jax.numpy as jnp
from jax import lax
from jax.experimental import pallas as pl
from jax.experimental.pallas import tpu as pltpu
from jax.sharding import PartitionSpec as P

sharpness = 10.0
shift = -4.0
multiplier = 262144.0
epsilon = 1e-06

F32, BF16 = jnp.float32, jnp.bfloat16


def dot(a, b, dims):
    return lax.dot_general(a, b, (dims, ((), ())), preferred_element_type=F32)


def nt(a, b):
    return dot(a, b, ((1,), (1,)))


def nn(a, b):
    return dot(a, b, ((1,), (0,)))


def up16(k):
    return -(-k // 16) * 16


def call(body, outs, scalars, arrays, us, alias=None):
    smem = pl.BlockSpec(memory_space=pltpu.SMEM)
    vmem = pl.BlockSpec(memory_space=pltpu.VMEM)
    return pl.pallas_call(
        body,
        out_shape=[jax.ShapeDtypeStruct(s, t) for s, t in outs],
        in_specs=[smem] * len(scalars) + [vmem] * len(arrays),
        out_specs=[vmem] * len(outs),
        input_output_aliases=alias or {},
        cost_estimate=pl.CostEstimate(
            flops=int(us * 2e8),
            transcendentals=0,
            bytes_accessed=sum(a.size * a.dtype.itemsize for a in arrays),
        ),
        compiler_params=pltpu.CompilerParams(vmem_limit_bytes=48 * 1024 * 1024),
    )(*scalars, *arrays)


def tie(xs):
    return lax.optimization_barrier(xs)


class Ring:
    def __init__(self, batch_size):
        n = self.n = batch_size // 2
        half = n // 2
        self.order = [2 * r if r < half else 2 * (n - 1 - r) + 1 for r in range(n)]
        self.fwd = self._perm(1)
        self.bwd = self._perm(-1)
        self.core = [(b, b ^ 1) for b in range(batch_size)]
        chip = lax.axis_index("batch") // 2
        self.pos = jnp.where(chip % 2 == 0, chip // 2, n - 1 - chip // 2)
        place = (self.pos + jnp.arange(n, dtype=jnp.int32)) % n
        self.chips = jnp.where(place < half, 2 * place, 2 * (n - 1 - place) + 1).astype(jnp.int32)

    def _perm(self, step):
        pairs = []
        for r, chip in enumerate(self.order):
            to = self.order[(r + step) % self.n]
            pairs += [(2 * chip + c, 2 * to + c) for c in range(2)]
        return pairs

    def right(self, x):
        return lax.ppermute(x, "batch", self.fwd)

    def left(self, x):
        return lax.ppermute(x, "batch", self.bwd)

    def other_core(self, x):
        return lax.ppermute(x, "batch", self.core)


def swap(x):
    return lax.ppermute(x, "tower", [(0, 1), (1, 0)])


def prepare(nb, ri, rt, rpi, rpt, core_ref, img_ref, txt_ref, ki_ref, gi_ref, kt_ref, gt_ref, *wide):
    first = core_ref[0] == 0
    rows = img_ref.shape[0]
    for feat, r, rp, keep, give in (
        (img_ref, ri, rpi, ki_ref, gi_ref),
        (txt_ref, rt, rpt, kt_ref, gt_ref),
    ):
        t = feat[...].T if r == rp else feat[...].astype(F32).T

        def block(b):
            x = t[b * r : (b + 1) * r]
            if rp > r:
                x = jnp.concatenate([x, jnp.zeros((rp - r, rows), x.dtype)])
            return x.astype(BF16)

        for q in range(nb // 2):
            a, b = block(2 * q), block(2 * q + 1)
            keep[q] = jnp.where(first, a, b)
            give[q] = jnp.where(first, b, a)
    for feat, r, rp, out in ((txt_ref, rt, rpt, wide[0]), (img_ref, ri, rpi, wide[-1])):
        if rp > r:
            out[...] = jnp.zeros_like(out)
            for b in range(nb):
                out[:, b * rp : b * rp + r] = feat[:, b * r : (b + 1) * r]


def feature_products(nb, ri, rt, final, s_ref, do_ref, dg_ref, wi_ref, wt_ref, *refs):
    image = s_ref[0] == 0
    do, dg = do_ref[...], dg_ref[...]
    dps = jnp.where(image, do, dg), jnp.where(image, dg, do)
    h = nb // 2
    base = (s_ref[0] if final else 1 - s_ref[0]) * h
    got, outs = refs[:-2], refs[-2:]
    for i, (dp, w_ref, r) in enumerate(((dps[0], wi_ref, ri), (dps[1], wt_ref, rt))):
        rp = w_ref.shape[1]
        if r == rp:
            x = nt(dp, w_ref[pl.ds(base, h)].reshape(h * r, dp.shape[1]))
        else:
            x = jnp.concatenate([nt(dp, w_ref[base + b])[:, :r] for b in range(h)], axis=1)
        if final:
            x = x + got[i][...].astype(F32)
        outs[i][...] = x.astype(BF16)


def project(n, rpi, rpt, rt, half, slot_ref, img_ref, txt_ref, *refs):
    chunks, (wi_ref, wt_ref, pi_ref, pt_ref, sq_ref, count_ref) = refs[:-6], refs[-6:]
    it = iter(chunks)
    h = n // 2
    for sibling in range(2):
        for d in range(n):
            b = slot_ref[sibling, d]
            if d == h:
                wi_ref[b] = next(it)[...]
                wt_ref[b] = next(it)[...]
            else:
                c = next(it)
                wi_ref[b] = c[:rpi]
                wt_ref[b] = c[rpi:]
    count_ref[...] = jnp.broadcast_to(
        sum(wt_ref[b, :, :128].astype(F32)[rt : rt + 1] for b in range(2 * n)), (8, 128)
    )
    pi = nn(img_ref[...], wi_ref[...].reshape(2 * n * rpi, half))
    pt = nn(txt_ref[...], wt_ref[...].reshape(2 * n * rpt, half))
    pi_ref[...] = pi
    pt_ref[...] = pt
    si = jnp.sum(pi * pi, axis=1, keepdims=True)
    st = jnp.sum(pt * pt, axis=1, keepdims=True)
    lane = lax.broadcasted_iota(jnp.int32, (pi.shape[0], 128), 1)
    sq_ref[...] = jnp.where(lane == 0, si, st).T[:8]


def normalize(s_ref, pi_ref, pt_ref, sq_ref, got_ref, mine_ref, other_ref, norm_ref):
    tower, valid = s_ref[0], s_ref[1]
    rows = pi_ref.shape[0]
    sq = sq_ref[...] + got_ref[...]
    norm = jnp.sqrt(sq + epsilon).T
    ni, nt_ = norm[:, 0:1], norm[:, 1:2]
    keep = lax.broadcasted_iota(jnp.int32, (rows, 1), 0) < valid
    u = jnp.where(keep, pi_ref[...] / ni, 0.0)
    v = jnp.where(keep, pt_ref[...] / nt_, 0.0)
    image = tower == 0
    mine_ref[...] = jnp.where(image, u, v).astype(BF16)
    other_ref[...] = jnp.where(image, v, u).astype(BF16)
    norm_ref[...] = jnp.where(image, ni, nt_)


def pairs(chunks, sides, first, *refs):
    half = refs[0].shape[1]
    m = len(sides)
    mine, refs = refs[: 2 * m], refs[2 * m :]
    fs, refs = refs[: 2 * chunks], refs[2 * chunks :]
    fo = jnp.concatenate([f[...] for f in fs[:chunks]]) if chunks > 1 else fs[0][...]
    fx = jnp.concatenate([f[...] for f in fs[chunks:]]) if chunks > 1 else fs[1][...]
    ins, outs = ((), refs) if first else (refs[:m], refs[m:])
    for i, side in enumerate(sides):
        mo, mx = mine[2 * i], mine[2 * i + 1]
        s = sharpness * (nt(mo[...], fo) + nt(mx[...], fx)) + shift
        if first and side == 0:
            r = lax.broadcasted_iota(jnp.int32, s.shape, 0)
            c = lax.broadcasted_iota(jnp.int32, s.shape, 1)
            g = jax.nn.sigmoid(jnp.where(r == c, -s, s))
            g = jnp.where(r == c, -g, g)
        else:
            g = jax.nn.sigmoid(s)
        qb = g.astype(BF16)
        for at, f in ((0, fo), (half, fx)):
            part = nn(qb, f)
            cols = slice(at, at + half)
            outs[i][:, cols] = (part if first else ins[i][:, cols] + part).astype(outs[i].dtype)


def back_norm(
    s_ref, count_ref, acc_ref, got_ref, last_ref, mo_ref, mx_ref, norm_ref, do_ref, dx_ref
):
    valid = s_ref[1]
    coef = sharpness * multiplier / count_ref[0:1, 0:1]
    rows, half = mo_ref.shape
    du = (acc_ref[...] + got_ref[...] + last_ref[...].astype(F32)) * coef
    duo, dux = du[:, :half], du[:, half:]
    mo, mx = mo_ref[...].astype(F32), mx_ref[...].astype(F32)
    along = jnp.sum(mo * duo, axis=1, keepdims=True) + jnp.sum(mx * dux, axis=1, keepdims=True)
    keep = lax.broadcasted_iota(jnp.int32, (rows, 1), 0) < valid
    norm = norm_ref[...]
    do_ref[...] = jnp.where(keep, (duo - mo * along) / norm, 0.0).astype(BF16)
    dx_ref[...] = jnp.where(keep, (dux - mx * along) / norm, 0.0).astype(BF16)


def products(n, first, s_ref, chip_ref, do_ref, dg_ref, so_ref, sg_ref, ai, bi, at, bt, *outs):
    image = s_ref[0] == 0
    do, dg, so, sg = do_ref[...], dg_ref[...], so_ref[...], sg_ref[...]
    img, img_s = jnp.where(image, do, dg), jnp.where(image, so, sg)
    txt, txt_s = jnp.where(image, dg, do), jnp.where(image, sg, so)
    rpi = ai.shape[1]
    h = n // 2
    for d in [h] if first else [d for d in range(n) if d != h]:
        q = chip_ref[d]
        gi = nn(ai[q], img) + nn(bi[q], img_s)
        gt = nn(at[q], txt) + nn(bt[q], txt_s)
        if first:
            outs[0][...] = gi.astype(BF16)
            outs[1][...] = gt.astype(BF16)
        else:
            outs[0][d, :rpi] = gi
            outs[0][d, rpi:] = gt


def shards(img_feat, txt_feat, img_proj, txt_proj, valid_rows):
    nb = lax.axis_size("batch")
    ring = Ring(nb)
    n, h = ring.n, ring.n // 2
    tower = lax.axis_index("tower")
    core = lax.axis_index("batch") % 2
    rows = img_feat.shape[0]
    ri, half = img_proj.shape
    rt = txt_proj.shape[0]
    rpi, rpt = up16(ri), up16(rt + 1)
    flags = jnp.stack([tower.astype(jnp.int32), valid_rows[0]])

    count_rows = jnp.broadcast_to(valid_rows.astype(BF16)[:, None], (rpt - rt, half))
    pad = jnp.zeros((rpi - ri, half), BF16)
    w = jnp.concatenate([img_proj] + [pad] * (rpi > ri) + [txt_proj, count_rows])
    prep = call(
        functools.partial(prepare, nb, ri, rt, rpi, rpt),
        [((n, rpi, rows), BF16)] * 2
        + [((n, rpt, rows), BF16)] * 2
        + [((rows, nb * rpt), BF16)]
        + [((rows, nb * rpi), BF16)] * (rpi > ri),
        [core.astype(jnp.int32).reshape(1)],
        [img_feat, txt_feat],
        1,
    )
    at = {0: w}
    sib = {0: ring.other_core(w)}
    f = b = w
    for k in range(1, h):
        f, b = ring.right(f), ring.left(b)
        if k == 1:
            f, b, *prep = tie((f, b, *prep))
        at[n - k], at[k] = f, b
        sib[n - k], sib[k] = ring.other_core(f), ring.other_core(b)
    img_keep, img_give, txt_keep, txt_give, txt_wide = prep[:5]
    img_wide = prep[5] if rpi > ri else img_feat
    f, b = ring.right(f[:rpi]), ring.left(b[rpi:])
    at[h], sib[h] = (f, b), (ring.other_core(f), ring.other_core(b))

    def flat(chunks):
        out = []
        for d in range(n):
            out += list(chunks[d]) if d == h else [chunks[d]]
        return out

    slots = jnp.stack([2 * ring.chips + core, 2 * ring.chips + 1 - core]).astype(jnp.int32)
    wi, wt, p_img, p_txt, sq, count = call(
        functools.partial(project, n, rpi, rpt, rt, half),
        [
            ((nb, rpi, half), BF16),
            ((nb, rpt, half), BF16),
            ((rows, half), F32),
            ((rows, half), F32),
            ((8, rows), F32),
            ((8, 128), F32),
        ],
        [slots],
        [img_wide, txt_wide] + flat(at) + flat(sib),
        4,
    )
    mine_o, other_o, norm = call(
        normalize,
        [((rows, half), BF16), ((rows, half), BF16), ((rows, 1), F32)],
        [flags],
        [p_img, p_txt, sq, swap(sq)],
        1,
    )

    other_x = swap(mine_o)
    other_x, late = tie((other_x, other_o))
    mine_x = swap(late)
    mine = [mine_o, mine_x, ring.other_core(mine_o), ring.other_core(mine_x)]

    def add(acc, sides, arrays, first=False, out=F32):
        chunks = len(arrays) // 2
        own = [a for side in sides for a in mine[2 * side : 2 * side + 2]]
        given = own + arrays
        return call(
            functools.partial(pairs, chunks, sides, first),
            [((rows, 2 * half), out)] * len(sides),
            [],
            given + list(acc),
            1.1 * len(sides),
            {len(given) + i: i for i in range(len(acc))},
        )

    acc = ()
    fa = ba = other_o
    fc = bc = other_x
    chunks = [[other_o, other_x]]
    cut = rows // 2
    for k in range(1, h + 1):
        if k == h:
            fa, ba, fc, bc = fa[:cut], ba[cut:], fc[:cut], bc[cut:]
        if k > 2 or k == h:
            j = k - 3
            if j >= 0:
                acc = add(acc, (0, 1), chunks[j], first=j == 0)
                fa, ba, *acc = tie((fa, ba, *acc))
        fa, ba = ring.right(fa), ring.left(ba)
        if k < h:
            fc, bc, fa, ba = tie((fc, bc, fa, ba))
        if k == h:
            acc = add(acc, (0, 1), chunks[h - 2], first=h == 2)
            fc, bc, *acc = tie((fc, bc, *acc))
        fc, bc = ring.right(fc), ring.left(bc)
        chunks.append([fa, ba, fc, bc])
    waiting = chunks[h - 1][:2] + chunks[h][:2] + chunks[h - 1][2:] + chunks[h][2:]
    got = ring.other_core(acc[1])
    (last,) = add((), (1,), waiting, first=True, out=BF16)
    last, *waiting = tie((last, *waiting))
    (mine_acc,) = add(acc[:1], (0,), waiting)
    dp_o, dp_x = call(
        back_norm,
        [((rows, half), BF16)] * 2,
        [flags],
        [count, mine_acc, got, ring.other_core(last), mine_o, mine_x, norm],
        1,
    )
    dp_got = swap(dp_x)
    dps = [dp_o, dp_got, ring.other_core(dp_o), ring.other_core(dp_got)]

    feats = [img_keep, ring.other_core(img_give), txt_keep, ring.other_core(txt_give)]

    def product(first, outs, ds):
        body = functools.partial(products, n, first)
        return call(body, outs, [flags, ring.chips], ds + feats, 1 if first else 2)

    f, b = product(True, [((rpi, half), BF16), ((rpt, half), BF16)], dps)
    dp_o, dp_got, f, b = tie((dp_o, dp_got, f, b))
    def grads(final, got):
        return call(
            functools.partial(feature_products, nb, ri, rt, final),
            [((rows, nb * ri // 2), BF16), ((rows, nb * rt // 2), BF16)],
            [flags],
            [dp_o, dp_got, wi, wt] + got,
            2,
        )

    (g,) = product(False, [((n, rpi + rpt, half), F32)], [dp_o, dp_got] + dps[2:])
    f, b = ring.right(f), ring.left(b)
    gives, got = grads(False, []), []
    for k in range(h - 1, 0, -1):
        pf, pb = g[k], g[n - k]
        if k == h - 1:
            f, b, *gives = tie((f, b, *gives))
            f = jnp.concatenate([pf[:rpi] + f.astype(F32), pf[rpi:]])
            b = jnp.concatenate([pb[:rpi], pb[rpi:] + b.astype(F32)])
        else:
            f, b = pf + f.astype(F32), pb + b.astype(F32)
        f, b = f.astype(BF16), b.astype(BF16)
        if k < h - 1 and gives:
            got.insert(0, swap(gives.pop()))
            f, b, got[0] = tie((f, b, got[0]))
        f, b = ring.right(f), ring.left(b)
    img_grad, txt_grad = grads(True, [swap(x) for x in gives] + got)
    f, b, img_grad, txt_grad = tie((f, b, img_grad, txt_grad))

    def total(lo, hi):
        return g[0, lo:hi] + f[lo:hi].astype(F32) + b[lo:hi].astype(F32)


    return (img_grad, txt_grad, total(0, ri), total(rpi, rpi + rt))


def solution(mesh):
    in_specs = (
        P("batch", None),
        P("batch", None),
        P("batch", "tower"),
        P("batch", "tower"),
        P("batch"),
    )
    out_specs = (P("batch", "tower"),) * 4
    return jax.shard_map(shards, mesh=mesh, in_specs=in_specs, out_specs=out_specs, check_vma=False)
```

```python
import functools

import jax
import jax.numpy as jnp
from jax import lax
from jax.experimental import pallas as pl
from jax.experimental.pallas import tpu as pltpu
from jax.sharding import PartitionSpec as P

sharpness = 10.0
shift = -4.0
multiplier = 262144.0
epsilon = 1e-06

F32, BF16 = jnp.float32, jnp.bfloat16


def dot(a, b, dims):
    return lax.dot_general(a, b, (dims, ((), ())), preferred_element_type=F32)


def nt(a, b):
    return dot(a, b, ((1,), (1,)))


def nn(a, b):
    return dot(a, b, ((1,), (0,)))


def up16(k):
    return -(-k // 16) * 16


def call(body, outs, scalars, arrays, us, alias=None):
    smem = pl.BlockSpec(memory_space=pltpu.SMEM)
    vmem = pl.BlockSpec(memory_space=pltpu.VMEM)
    return pl.pallas_call(
        body,
        out_shape=[jax.ShapeDtypeStruct(s, t) for s, t in outs],
        in_specs=[smem] * len(scalars) + [vmem] * len(arrays),
        out_specs=[vmem] * len(outs),
        input_output_aliases=alias or {},
        cost_estimate=pl.CostEstimate(
            flops=int(us * 2e8),
            transcendentals=0,
            bytes_accessed=sum(a.size * a.dtype.itemsize for a in arrays),
        ),
        compiler_params=pltpu.CompilerParams(vmem_limit_bytes=48 * 1024 * 1024),
    )(*scalars, *arrays)


def tie(xs):
    return lax.optimization_barrier(xs)


class Ring:
    def __init__(self, batch_size):
        n = self.n = batch_size // 2
        half = n // 2
        self.order = [2 * r if r < half else 2 * (n - 1 - r) + 1 for r in range(n)]
        self.fwd = self._perm(1)
        self.bwd = self._perm(-1)
        self.core = [(b, b ^ 1) for b in range(batch_size)]
        chip = lax.axis_index("batch") // 2
        self.pos = jnp.where(chip % 2 == 0, chip // 2, n - 1 - chip // 2)
        place = (self.pos + jnp.arange(n, dtype=jnp.int32)) % n
        self.chips = jnp.where(place < half, 2 * place, 2 * (n - 1 - place) + 1).astype(jnp.int32)

    def _perm(self, step):
        pairs = []
        for r, chip in enumerate(self.order):
            to = self.order[(r + step) % self.n]
            pairs += [(2 * chip + c, 2 * to + c) for c in range(2)]
        return pairs

    def right(self, x):
        return lax.ppermute(x, "batch", self.fwd)

    def left(self, x):
        return lax.ppermute(x, "batch", self.bwd)

    def other_core(self, x):
        return lax.ppermute(x, "batch", self.core)


def swap(x):
    return lax.ppermute(x, "tower", [(0, 1), (1, 0)])


def prepare(nb, ri, rt, rpi, rpt, core_ref, img_ref, txt_ref, ki_ref, gi_ref, kt_ref, gt_ref, *wide):
    first = core_ref[0] == 0
    rows = img_ref.shape[0]
    for feat, r, rp, keep, give in (
        (img_ref, ri, rpi, ki_ref, gi_ref),
        (txt_ref, rt, rpt, kt_ref, gt_ref),
    ):
        t = feat[...].T if r == rp else feat[...].astype(F32).T

        def block(b):
            x = t[b * r : (b + 1) * r]
            if rp > r:
                x = jnp.concatenate([x, jnp.zeros((rp - r, rows), x.dtype)])
            return x.astype(BF16)

        for q in range(nb // 2):
            a, b = block(2 * q), block(2 * q + 1)
            keep[q] = jnp.where(first, a, b)
            give[q] = jnp.where(first, b, a)
    for feat, r, rp, out in ((txt_ref, rt, rpt, wide[0]), (img_ref, ri, rpi, wide[-1])):
        if rp > r:
            out[...] = jnp.zeros_like(out)
            for b in range(nb):
                out[:, b * rp : b * rp + r] = feat[:, b * r : (b + 1) * r]


def feature_products(nb, ri, rt, s_ref, do_ref, dg_ref, wi_ref, wt_ref, keep_ref, give_ref):
    image = s_ref[0] == 0
    do, dg = do_ref[...], dg_ref[...]
    dps = jnp.where(image, do, dg), jnp.where(image, dg, do)
    h = nb // 2
    for out, tower in ((give_ref, 1 - s_ref[0]), (keep_ref, s_ref[0])):
        at = 0
        for dp, w_ref, r in ((dps[0], wi_ref, ri), (dps[1], wt_ref, rt)):
            if r == w_ref.shape[1]:
                x = nt(dp, w_ref[pl.ds(tower * h, h)].reshape(h * r, dp.shape[1]))
            else:
                x = [nt(dp, w_ref[tower * h + b])[:, :r] for b in range(h)]
                x = jnp.concatenate(x, axis=1)
            out[:, at : at + h * r] = x.astype(out.dtype)
            at += h * r


def finish(keep_ref, got_ref, img_ref, txt_ref):
    at = 0
    for out in (img_ref, txt_ref):
        cols = slice(at, at + out.shape[1])
        out[...] = (keep_ref[:, cols] + got_ref[:, cols].astype(F32)).astype(BF16)
        at += out.shape[1]


def project(n, rpi, rpt, rt, half, slot_ref, img_ref, txt_ref, *refs):
    chunks, (wi_ref, wt_ref, pi_ref, pt_ref, sq_ref, count_ref) = refs[:-6], refs[-6:]
    it = iter(chunks)
    h = n // 2
    for sibling in range(2):
        for d in range(n):
            b = slot_ref[sibling, d]
            if d == h:
                wi_ref[b] = next(it)[...]
                wt_ref[b] = next(it)[...]
            else:
                c = next(it)
                wi_ref[b] = c[:rpi]
                wt_ref[b] = c[rpi:]
    count_ref[...] = jnp.broadcast_to(
        sum(wt_ref[b, :, :128].astype(F32)[rt : rt + 1] for b in range(2 * n)), (8, 128)
    )
    pi = nn(img_ref[...], wi_ref[...].reshape(2 * n * rpi, half))
    pt = nn(txt_ref[...], wt_ref[...].reshape(2 * n * rpt, half))
    pi_ref[...] = pi
    pt_ref[...] = pt
    si = jnp.sum(pi * pi, axis=1, keepdims=True)
    st = jnp.sum(pt * pt, axis=1, keepdims=True)
    lane = lax.broadcasted_iota(jnp.int32, (pi.shape[0], 128), 1)
    sq_ref[...] = jnp.where(lane == 0, si, st).T[:8]


def normalize(s_ref, pi_ref, pt_ref, sq_ref, got_ref, mine_ref, other_ref, norm_ref):
    tower, valid = s_ref[0], s_ref[1]
    rows = pi_ref.shape[0]
    sq = sq_ref[...] + got_ref[...]
    norm = jnp.sqrt(sq + epsilon).T
    ni, nt_ = norm[:, 0:1], norm[:, 1:2]
    keep = lax.broadcasted_iota(jnp.int32, (rows, 1), 0) < valid
    u = jnp.where(keep, pi_ref[...] / ni, 0.0)
    v = jnp.where(keep, pt_ref[...] / nt_, 0.0)
    image = tower == 0
    mine_ref[...] = jnp.where(image, u, v).astype(BF16)
    other_ref[...] = jnp.where(image, v, u).astype(BF16)
    norm_ref[...] = jnp.where(image, ni, nt_)


def pairs(chunks, sides, first, *refs):
    half = refs[0].shape[1]
    m = len(sides)
    mine, refs = refs[: 2 * m], refs[2 * m :]
    fs, refs = refs[: 2 * chunks], refs[2 * chunks :]
    fo = jnp.concatenate([f[...] for f in fs[:chunks]]) if chunks > 1 else fs[0][...]
    fx = jnp.concatenate([f[...] for f in fs[chunks:]]) if chunks > 1 else fs[1][...]
    ins, outs = ((), refs) if first else (refs[:m], refs[m:])
    for i, side in enumerate(sides):
        mo, mx = mine[2 * i], mine[2 * i + 1]
        s = sharpness * (nt(mo[...], fo) + nt(mx[...], fx)) + shift
        if first and side == 0:
            r = lax.broadcasted_iota(jnp.int32, s.shape, 0)
            c = lax.broadcasted_iota(jnp.int32, s.shape, 1)
            g = jax.nn.sigmoid(jnp.where(r == c, -s, s))
            g = jnp.where(r == c, -g, g)
        else:
            g = jax.nn.sigmoid(s)
        qb = g.astype(BF16)
        for at, f in ((0, fo), (half, fx)):
            part = nn(qb, f)
            cols = slice(at, at + half)
            outs[i][:, cols] = (part if first else ins[i][:, cols] + part).astype(outs[i].dtype)


def back_norm(
    s_ref, count_ref, acc_ref, got_ref, last_ref, mo_ref, mx_ref, norm_ref, do_ref, dx_ref
):
    valid = s_ref[1]
    coef = sharpness * multiplier / count_ref[0:1, 0:1]
    rows, half = mo_ref.shape
    du = (acc_ref[...] + got_ref[...] + last_ref[...].astype(F32)) * coef
    duo, dux = du[:, :half], du[:, half:]
    mo, mx = mo_ref[...].astype(F32), mx_ref[...].astype(F32)
    along = jnp.sum(mo * duo, axis=1, keepdims=True) + jnp.sum(mx * dux, axis=1, keepdims=True)
    keep = lax.broadcasted_iota(jnp.int32, (rows, 1), 0) < valid
    norm = norm_ref[...]
    do_ref[...] = jnp.where(keep, (duo - mo * along) / norm, 0.0).astype(BF16)
    dx_ref[...] = jnp.where(keep, (dux - mx * along) / norm, 0.0).astype(BF16)


def products(n, first, s_ref, chip_ref, do_ref, dg_ref, so_ref, sg_ref, ai, bi, at, bt, *outs):
    image = s_ref[0] == 0
    do, dg, so, sg = do_ref[...], dg_ref[...], so_ref[...], sg_ref[...]
    img, img_s = jnp.where(image, do, dg), jnp.where(image, so, sg)
    txt, txt_s = jnp.where(image, dg, do), jnp.where(image, sg, so)
    rpi = ai.shape[1]
    h = n // 2
    early = [h, h - 1, n - h + 1]
    for d in early if first else [d for d in range(n) if d not in early]:
        q = chip_ref[d]
        gi = nn(ai[q], img) + nn(bi[q], img_s)
        gt = nn(at[q], txt) + nn(bt[q], txt_s)
        if d == h:
            outs[0][...] = gi.astype(BF16)
            outs[1][...] = gt.astype(BF16)
        else:
            out = outs[1 + early.index(d)] if first else outs[0].at[d]
            out[:rpi] = gi
            out[rpi:] = gt


def shards(img_feat, txt_feat, img_proj, txt_proj, valid_rows):
    nb = lax.axis_size("batch")
    ring = Ring(nb)
    n, h = ring.n, ring.n // 2
    tower = lax.axis_index("tower")
    core = lax.axis_index("batch") % 2
    rows = img_feat.shape[0]
    ri, half = img_proj.shape
    rt = txt_proj.shape[0]
    rpi, rpt = up16(ri), up16(rt + 1)
    flags = jnp.stack([tower.astype(jnp.int32), valid_rows[0]])

    count_rows = jnp.broadcast_to(valid_rows.astype(BF16)[:, None], (rpt - rt, half))
    pad = jnp.zeros((rpi - ri, half), BF16)
    w = jnp.concatenate([img_proj] + [pad] * (rpi > ri) + [txt_proj, count_rows])
    prep = call(
        functools.partial(prepare, nb, ri, rt, rpi, rpt),
        [((n, rpi, rows), BF16)] * 2
        + [((n, rpt, rows), BF16)] * 2
        + [((rows, nb * rpt), BF16)]
        + [((rows, nb * rpi), BF16)] * (rpi > ri),
        [core.astype(jnp.int32).reshape(1)],
        [img_feat, txt_feat],
        1,
    )
    at = {0: w}
    sib = {0: ring.other_core(w)}
    f = b = w
    for k in range(1, h):
        f, b = ring.right(f), ring.left(b)
        if k == 1:
            f, b, *prep = tie((f, b, *prep))
        at[n - k], at[k] = f, b
        sib[n - k], sib[k] = ring.other_core(f), ring.other_core(b)
    img_keep, img_give, txt_keep, txt_give, txt_wide = prep[:5]
    img_wide = prep[5] if rpi > ri else img_feat
    f, b = ring.right(f[:rpi]), ring.left(b[rpi:])
    at[h], sib[h] = (f, b), (ring.other_core(f), ring.other_core(b))

    def flat(chunks):
        out = []
        for d in range(n):
            out += list(chunks[d]) if d == h else [chunks[d]]
        return out

    slots = jnp.stack([2 * ring.chips + core, 2 * ring.chips + 1 - core]).astype(jnp.int32)
    wi, wt, p_img, p_txt, sq, count = call(
        functools.partial(project, n, rpi, rpt, rt, half),
        [
            ((nb, rpi, half), BF16),
            ((nb, rpt, half), BF16),
            ((rows, half), F32),
            ((rows, half), F32),
            ((8, rows), F32),
            ((8, 128), F32),
        ],
        [slots],
        [img_wide, txt_wide] + flat(at) + flat(sib),
        4,
    )
    mine_o, other_o, norm = call(
        normalize,
        [((rows, half), BF16), ((rows, half), BF16), ((rows, 1), F32)],
        [flags],
        [p_img, p_txt, sq, swap(sq)],
        1,
    )

    other_x = swap(mine_o)
    other_x, late = tie((other_x, other_o))
    mine_x = swap(late)
    mine = [mine_o, mine_x, ring.other_core(mine_o), ring.other_core(mine_x)]

    def add(acc, sides, arrays, first=False, out=F32):
        chunks = len(arrays) // 2
        own = [a for side in sides for a in mine[2 * side : 2 * side + 2]]
        given = own + arrays
        return call(
            functools.partial(pairs, chunks, sides, first),
            [((rows, 2 * half), out)] * len(sides),
            [],
            given + list(acc),
            1.1 * len(sides),
            {len(given) + i: i for i in range(len(acc))},
        )

    acc = ()
    fa = ba = other_o
    fc = bc = other_x
    chunks = [[other_o, other_x]]
    cut = rows // 2
    for k in range(1, h + 1):
        if k == h:
            fa, ba, fc, bc = fa[:cut], ba[cut:], fc[:cut], bc[cut:]
        if k > 2 or k == h:
            j = k - 3
            if j >= 0:
                acc = add(acc, (0, 1), chunks[j], first=j == 0)
                fa, ba, *acc = tie((fa, ba, *acc))
        fa, ba = ring.right(fa), ring.left(ba)
        if k < h:
            fc, bc, fa, ba = tie((fc, bc, fa, ba))
        if k == h:
            acc = add(acc, (0, 1), chunks[h - 2], first=h == 2)
            fc, bc, *acc = tie((fc, bc, *acc))
        fc, bc = ring.right(fc), ring.left(bc)
        chunks.append([fa, ba, fc, bc])
    waiting = chunks[h - 1][:2] + chunks[h][:2] + chunks[h - 1][2:] + chunks[h][2:]
    got = ring.other_core(acc[1])
    (last,) = add((), (1,), waiting, first=True, out=BF16)
    last, *waiting = tie((last, *waiting))
    (mine_acc,) = add(acc[:1], (0,), waiting)
    dp_o, dp_x = call(
        back_norm,
        [((rows, half), BF16)] * 2,
        [flags],
        [count, mine_acc, got, ring.other_core(last), mine_o, mine_x, norm],
        1,
    )
    dp_got = swap(dp_x)
    dps = [dp_o, dp_got, ring.other_core(dp_o), ring.other_core(dp_got)]

    feats = [img_keep, ring.other_core(img_give), txt_keep, ring.other_core(txt_give)]

    def product(first, outs, ds):
        body = functools.partial(products, n, first)
        return call(body, outs, [flags, ring.chips], ds + feats, 1 if first else 2)

    chunk = ((rpi + rpt, half), F32)
    f, b, gf, gb = product(True, [((rpi, half), BF16), ((rpt, half), BF16), chunk, chunk], dps)
    dp_o, dp_got, f, b = tie((dp_o, dp_got, f, b))
    keep, give = call(
        functools.partial(feature_products, nb, ri, rt),
        [((rows, nb * (ri + rt) // 2), F32), ((rows, nb * (ri + rt) // 2), BF16)],
        [flags],
        [dp_o, dp_got, wi, wt],
        3,
    )

    f, b = ring.right(f), ring.left(b)
    f, *late = tie((f, *dps))
    (g,) = product(False, [((n, rpi + rpt, half), F32)], late)
    for k in range(h - 1, 0, -1):
        pf, pb = (gf, gb) if k == h - 1 else (g[k], g[n - k])
        if k == h - 1:
            f = jnp.concatenate([pf[:rpi] + f.astype(F32), pf[rpi:]])
            b = jnp.concatenate([pb[:rpi], pb[rpi:] + b.astype(F32)])
        else:
            f, b = pf + f.astype(F32), pb + b.astype(F32)
        f, b = f.astype(BF16), b.astype(BF16)
        if k == h - 2:
            f, b, keep, give = tie((f, b, keep, give))
        f, b = ring.right(f), ring.left(b)
    got = swap(give)
    img_grad, txt_grad = call(
        finish,
        [((rows, nb * r // 2), BF16) for r in (ri, rt)],
        [],
        [keep, got],
        10,
    )
    f, b, img_grad, txt_grad = tie((f, b, img_grad, txt_grad))

    def total(lo, hi):
        return g[0, lo:hi] + f[lo:hi].astype(F32) + b[lo:hi].astype(F32)

    img_total, txt_total = total(0, ri), total(rpi, rpi + rt)
    return img_grad, txt_grad, img_total, txt_total


def solution(mesh):
    in_specs = (
        P("batch", None),
        P("batch", None),
        P("batch", "tower"),
        P("batch", "tower"),
        P("batch"),
    )
    out_specs = (P("batch", "tower"),) * 4
    return jax.shard_map(shards, mesh=mesh, in_specs=in_specs, out_specs=out_specs, check_vma=False)
```

```python
import functools

import jax
import jax.numpy as jnp
from jax import lax
from jax.experimental import pallas as pl
from jax.experimental.pallas import tpu as pltpu
from jax.sharding import PartitionSpec as P

sharpness = 10.0
shift = -4.0
multiplier = 262144.0
epsilon = 1e-06

F32, BF16 = jnp.float32, jnp.bfloat16


def dot(a, b, dims):
    return lax.dot_general(a, b, (dims, ((), ())), preferred_element_type=F32)


def nt(a, b):
    return dot(a, b, ((1,), (1,)))


def nn(a, b):
    return dot(a, b, ((1,), (0,)))


def up16(k):
    return -(-k // 16) * 16


def call(body, outs, scalars, arrays, us, alias=None):
    smem = pl.BlockSpec(memory_space=pltpu.SMEM)
    vmem = pl.BlockSpec(memory_space=pltpu.VMEM)
    return pl.pallas_call(
        body,
        out_shape=[jax.ShapeDtypeStruct(s, t) for s, t in outs],
        in_specs=[smem] * len(scalars) + [vmem] * len(arrays),
        out_specs=[vmem] * len(outs),
        input_output_aliases=alias or {},
        cost_estimate=pl.CostEstimate(
            flops=int(us * 2e8),
            transcendentals=0,
            bytes_accessed=sum(a.size * a.dtype.itemsize for a in arrays),
        ),
        compiler_params=pltpu.CompilerParams(vmem_limit_bytes=48 * 1024 * 1024),
    )(*scalars, *arrays)


def tie(xs):
    return lax.optimization_barrier(xs)


class Ring:
    def __init__(self, batch_size):
        n = self.n = batch_size // 2
        half = n // 2
        self.order = [2 * r if r < half else 2 * (n - 1 - r) + 1 for r in range(n)]
        self.fwd = self._perm(1)
        self.bwd = self._perm(-1)
        self.core = [(b, b ^ 1) for b in range(batch_size)]
        chip = lax.axis_index("batch") // 2
        self.pos = jnp.where(chip % 2 == 0, chip // 2, n - 1 - chip // 2)
        place = (self.pos + jnp.arange(n, dtype=jnp.int32)) % n
        self.chips = jnp.where(place < half, 2 * place, 2 * (n - 1 - place) + 1).astype(jnp.int32)

    def _perm(self, step):
        pairs = []
        for r, chip in enumerate(self.order):
            to = self.order[(r + step) % self.n]
            pairs += [(2 * chip + c, 2 * to + c) for c in range(2)]
        return pairs

    def right(self, x):
        return lax.ppermute(x, "batch", self.fwd)

    def left(self, x):
        return lax.ppermute(x, "batch", self.bwd)

    def other_core(self, x):
        return lax.ppermute(x, "batch", self.core)


def swap(x):
    return lax.ppermute(x, "tower", [(0, 1), (1, 0)])


def prepare(nb, ri, rt, rpi, rpt, core_ref, img_ref, txt_ref, ki_ref, gi_ref, kt_ref, gt_ref, *wide):
    first = core_ref[0] == 0
    rows = img_ref.shape[0]
    for feat, r, rp, keep, give in (
        (img_ref, ri, rpi, ki_ref, gi_ref),
        (txt_ref, rt, rpt, kt_ref, gt_ref),
    ):
        t = feat[...].T if r == rp else feat[...].astype(F32).T

        def block(b):
            x = t[b * r : (b + 1) * r]
            if rp > r:
                x = jnp.concatenate([x, jnp.zeros((rp - r, rows), x.dtype)])
            return x.astype(BF16)

        for q in range(nb // 2):
            a, b = block(2 * q), block(2 * q + 1)
            keep[q] = jnp.where(first, a, b)
            give[q] = jnp.where(first, b, a)
    for feat, r, rp, out in ((txt_ref, rt, rpt, wide[0]), (img_ref, ri, rpi, wide[-1])):
        if rp > r:
            out[...] = jnp.zeros_like(out)
            for b in range(nb):
                out[:, b * rp : b * rp + r] = feat[:, b * r : (b + 1) * r]


def feature_products(nb, ri, rt, s_ref, do_ref, dg_ref, wi_ref, wt_ref, keep_ref, give_ref):
    image = s_ref[0] == 0
    do, dg = do_ref[...], dg_ref[...]
    dps = jnp.where(image, do, dg), jnp.where(image, dg, do)
    h = nb // 2
    for out, tower in ((give_ref, 1 - s_ref[0]), (keep_ref, s_ref[0])):
        at = 0
        for dp, w_ref, r in ((dps[0], wi_ref, ri), (dps[1], wt_ref, rt)):
            if r == w_ref.shape[1]:
                x = nt(dp, w_ref[pl.ds(tower * h, h)].reshape(h * r, dp.shape[1]))
            else:
                x = [nt(dp, w_ref[tower * h + b])[:, :r] for b in range(h)]
                x = jnp.concatenate(x, axis=1)
            out[:, at : at + h * r] = x.astype(out.dtype)
            at += h * r


def finish(keep_ref, got_ref, img_ref, txt_ref):
    at = 0
    for out in (img_ref, txt_ref):
        cols = slice(at, at + out.shape[1])
        out[...] = (keep_ref[:, cols] + got_ref[:, cols].astype(F32)).astype(BF16)
        at += out.shape[1]


def project(n, rpi, rpt, rt, half, slot_ref, img_ref, txt_ref, *refs):
    chunks, (wi_ref, wt_ref, pi_ref, pt_ref, sq_ref, count_ref) = refs[:-6], refs[-6:]
    it = iter(chunks)
    h = n // 2
    for sibling in range(2):
        for d in range(n):
            b = slot_ref[sibling, d]
            if d == h:
                wi_ref[b] = next(it)[...]
                wt_ref[b] = next(it)[...]
            else:
                c = next(it)
                wi_ref[b] = c[:rpi]
                wt_ref[b] = c[rpi:]
    count_ref[...] = jnp.broadcast_to(
        sum(wt_ref[b, :, :128].astype(F32)[rt : rt + 1] for b in range(2 * n)), (8, 128)
    )
    pi = nn(img_ref[...], wi_ref[...].reshape(2 * n * rpi, half))
    pt = nn(txt_ref[...], wt_ref[...].reshape(2 * n * rpt, half))
    pi_ref[...] = pi
    pt_ref[...] = pt
    si = jnp.sum(pi * pi, axis=1, keepdims=True)
    st = jnp.sum(pt * pt, axis=1, keepdims=True)
    lane = lax.broadcasted_iota(jnp.int32, (pi.shape[0], 128), 1)
    sq_ref[...] = jnp.where(lane == 0, si, st).T[:8]


def normalize(s_ref, pi_ref, pt_ref, sq_ref, got_ref, mine_ref, other_ref, norm_ref):
    tower, valid = s_ref[0], s_ref[1]
    rows = pi_ref.shape[0]
    sq = sq_ref[...] + got_ref[...]
    norm = jnp.sqrt(sq + epsilon).T
    ni, nt_ = norm[:, 0:1], norm[:, 1:2]
    keep = lax.broadcasted_iota(jnp.int32, (rows, 1), 0) < valid
    u = jnp.where(keep, pi_ref[...] / ni, 0.0)
    v = jnp.where(keep, pt_ref[...] / nt_, 0.0)
    image = tower == 0
    mine_ref[...] = jnp.where(image, u, v).astype(BF16)
    other_ref[...] = jnp.where(image, v, u).astype(BF16)
    norm_ref[...] = jnp.where(image, ni, nt_)


def pairs(chunks, sides, first, *refs):
    half = refs[0].shape[1]
    m = len(sides)
    mine, refs = refs[: 2 * m], refs[2 * m :]
    fs, refs = refs[: 2 * chunks], refs[2 * chunks :]
    fo = jnp.concatenate([f[...] for f in fs[:chunks]]) if chunks > 1 else fs[0][...]
    fx = jnp.concatenate([f[...] for f in fs[chunks:]]) if chunks > 1 else fs[1][...]
    ins, outs = ((), refs) if first else (refs[:m], refs[m:])
    for i, side in enumerate(sides):
        mo, mx = mine[2 * i], mine[2 * i + 1]
        s = sharpness * (nt(mo[...], fo) + nt(mx[...], fx)) + shift
        if first and side == 0:
            r = lax.broadcasted_iota(jnp.int32, s.shape, 0)
            c = lax.broadcasted_iota(jnp.int32, s.shape, 1)
            g = jax.nn.sigmoid(jnp.where(r == c, -s, s))
            g = jnp.where(r == c, -g, g)
        else:
            g = jax.nn.sigmoid(s)
        qb = g.astype(BF16)
        for at, f in ((0, fo), (half, fx)):
            part = nn(qb, f)
            cols = slice(at, at + half)
            outs[i][:, cols] = (part if first else ins[i][:, cols] + part).astype(outs[i].dtype)


def back_norm(
    s_ref, count_ref, acc_ref, got_ref, last_ref, mo_ref, mx_ref, norm_ref, do_ref, dx_ref
):
    valid = s_ref[1]
    coef = sharpness * multiplier / count_ref[0:1, 0:1]
    rows, half = mo_ref.shape
    du = (acc_ref[...] + got_ref[...] + last_ref[...].astype(F32)) * coef
    duo, dux = du[:, :half], du[:, half:]
    mo, mx = mo_ref[...].astype(F32), mx_ref[...].astype(F32)
    along = jnp.sum(mo * duo, axis=1, keepdims=True) + jnp.sum(mx * dux, axis=1, keepdims=True)
    keep = lax.broadcasted_iota(jnp.int32, (rows, 1), 0) < valid
    norm = norm_ref[...]
    do_ref[...] = jnp.where(keep, (duo - mo * along) / norm, 0.0).astype(BF16)
    dx_ref[...] = jnp.where(keep, (dux - mx * along) / norm, 0.0).astype(BF16)


def products(n, first, s_ref, chip_ref, do_ref, dg_ref, so_ref, sg_ref, ai, bi, at, bt, *outs):
    image = s_ref[0] == 0
    do, dg, so, sg = do_ref[...], dg_ref[...], so_ref[...], sg_ref[...]
    img, img_s = jnp.where(image, do, dg), jnp.where(image, so, sg)
    txt, txt_s = jnp.where(image, dg, do), jnp.where(image, sg, so)
    rpi = ai.shape[1]
    h = n // 2
    early = [h, h - 1, n - h + 1]
    for d in early if first else [d for d in range(n) if d not in early]:
        q = chip_ref[d]
        gi = nn(ai[q], img) + nn(bi[q], img_s)
        gt = nn(at[q], txt) + nn(bt[q], txt_s)
        if d == h:
            outs[0][...] = gi.astype(BF16)
            outs[1][...] = gt.astype(BF16)
        else:
            out = outs[1 + early.index(d)] if first else outs[0].at[d]
            out[:rpi] = gi
            out[rpi:] = gt


def shards(img_feat, txt_feat, img_proj, txt_proj, valid_rows):
    nb = lax.axis_size("batch")
    ring = Ring(nb)
    n, h = ring.n, ring.n // 2
    tower = lax.axis_index("tower")
    core = lax.axis_index("batch") % 2
    rows = img_feat.shape[0]
    ri, half = img_proj.shape
    rt = txt_proj.shape[0]
    rpi, rpt = up16(ri), up16(rt + 1)
    flags = jnp.stack([tower.astype(jnp.int32), valid_rows[0]])

    count_rows = jnp.broadcast_to(valid_rows.astype(BF16)[:, None], (rpt - rt, half))
    pad = jnp.zeros((rpi - ri, half), BF16)
    w = jnp.concatenate([img_proj] + [pad] * (rpi > ri) + [txt_proj, count_rows])
    prep = call(
        functools.partial(prepare, nb, ri, rt, rpi, rpt),
        [((n, rpi, rows), BF16)] * 2
        + [((n, rpt, rows), BF16)] * 2
        + [((rows, nb * rpt), BF16)]
        + [((rows, nb * rpi), BF16)] * (rpi > ri),
        [core.astype(jnp.int32).reshape(1)],
        [img_feat, txt_feat],
        1,
    )
    at = {0: w}
    sib = {0: ring.other_core(w)}
    f = b = w
    for k in range(1, h):
        f, b = ring.right(f), ring.left(b)
        if k == 1:
            f, b, *prep = tie((f, b, *prep))
        at[n - k], at[k] = f, b
        sib[n - k], sib[k] = ring.other_core(f), ring.other_core(b)
    img_keep, img_give, txt_keep, txt_give, txt_wide = prep[:5]
    img_wide = prep[5] if rpi > ri else img_feat
    f, b = ring.right(f[:rpi]), ring.left(b[rpi:])
    at[h], sib[h] = (f, b), (ring.other_core(f), ring.other_core(b))

    def flat(chunks):
        out = []
        for d in range(n):
            out += list(chunks[d]) if d == h else [chunks[d]]
        return out

    slots = jnp.stack([2 * ring.chips + core, 2 * ring.chips + 1 - core]).astype(jnp.int32)
    wi, wt, p_img, p_txt, sq, count = call(
        functools.partial(project, n, rpi, rpt, rt, half),
        [
            ((nb, rpi, half), BF16),
            ((nb, rpt, half), BF16),
            ((rows, half), F32),
            ((rows, half), F32),
            ((8, rows), F32),
            ((8, 128), F32),
        ],
        [slots],
        [img_wide, txt_wide] + flat(at) + flat(sib),
        4,
    )
    mine_o, other_o, norm = call(
        normalize,
        [((rows, half), BF16), ((rows, half), BF16), ((rows, 1), F32)],
        [flags],
        [p_img, p_txt, sq, swap(sq)],
        1,
    )

    other_x = swap(mine_o)
    other_x, late = tie((other_x, other_o))
    mine_x = swap(late)
    mine = [mine_o, mine_x, ring.other_core(mine_o), ring.other_core(mine_x)]

    def add(acc, sides, arrays, first=False, out=F32):
        chunks = len(arrays) // 2
        own = [a for side in sides for a in mine[2 * side : 2 * side + 2]]
        given = own + arrays
        return call(
            functools.partial(pairs, chunks, sides, first),
            [((rows, 2 * half), out)] * len(sides),
            [],
            given + list(acc),
            1.1 * len(sides),
            {len(given) + i: i for i in range(len(acc))},
        )

    acc = ()
    fa = ba = other_o
    fc = bc = other_x
    chunks = [[other_o, other_x]]
    cut = rows // 2
    for k in range(1, h + 1):
        if k == h:
            fa, ba, fc, bc = fa[:cut], ba[cut:], fc[:cut], bc[cut:]
        if 2 < k < h:
            acc = add(acc, (0, 1), chunks[k - 3], first=k == 3)
            fa, ba, *acc = tie((fa, ba, *acc))
        fa, ba = ring.right(fa), ring.left(ba)
        fc, bc, fa, ba = tie((fc, bc, fa, ba))
        if k > max(1, h - 2):
            acc = add(acc, (0, 1), chunks[k - 2], first=k == 2)
            fc, bc, *acc = tie((fc, bc, *acc))
        fc, bc = ring.right(fc), ring.left(bc)
        chunks.append([fa, ba, fc, bc])
    waiting = chunks[h - 1][:2] + chunks[h][:2] + chunks[h - 1][2:] + chunks[h][2:]
    got = ring.other_core(acc[1])
    (last,) = add((), (1,), waiting, first=True, out=BF16)
    last, *waiting = tie((last, *waiting))
    (mine_acc,) = add(acc[:1], (0,), waiting)
    dp_o, dp_x = call(
        back_norm,
        [((rows, half), BF16)] * 2,
        [flags],
        [count, mine_acc, got, ring.other_core(last), mine_o, mine_x, norm],
        1,
    )
    dp_got = swap(dp_x)
    dps = [dp_o, dp_got, ring.other_core(dp_o), ring.other_core(dp_got)]

    feats = [img_keep, ring.other_core(img_give), txt_keep, ring.other_core(txt_give)]

    def product(first, outs, ds):
        body = functools.partial(products, n, first)
        return call(body, outs, [flags, ring.chips], ds + feats, 1 if first else 2)

    chunk = ((rpi + rpt, half), F32)
    f, b, gf, gb = product(True, [((rpi, half), BF16), ((rpt, half), BF16), chunk, chunk], dps)
    dp_o, dp_got, f, b = tie((dp_o, dp_got, f, b))
    keep, give = call(
        functools.partial(feature_products, nb, ri, rt),
        [((rows, nb * (ri + rt) // 2), F32), ((rows, nb * (ri + rt) // 2), BF16)],
        [flags],
        [dp_o, dp_got, wi, wt],
        3,
    )

    f, b = ring.right(f), ring.left(b)
    f, *late = tie((f, *dps))
    (g,) = product(False, [((n, rpi + rpt, half), F32)], late)
    for k in range(h - 1, 0, -1):
        pf, pb = (gf, gb) if k == h - 1 else (g[k], g[n - k])
        if k == h - 1:
            f = jnp.concatenate([pf[:rpi] + f.astype(F32), pf[rpi:]])
            b = jnp.concatenate([pb[:rpi], pb[rpi:] + b.astype(F32)])
        else:
            f, b = pf + f.astype(F32), pb + b.astype(F32)
        f, b = f.astype(BF16), b.astype(BF16)
        if k == h - 2:
            f, b, keep, give = tie((f, b, keep, give))
        f, b = ring.right(f), ring.left(b)
    got = swap(give)
    img_grad, txt_grad = call(
        finish,
        [((rows, nb * r // 2), BF16) for r in (ri, rt)],
        [],
        [keep, got],
        10,
    )
    f, b, img_grad, txt_grad = tie((f, b, img_grad, txt_grad))

    def total(lo, hi):
        return g[0, lo:hi] + f[lo:hi].astype(F32) + b[lo:hi].astype(F32)

    img_total, txt_total = total(0, ri), total(rpi, rpi + rt)
    return img_grad, txt_grad, img_total, txt_total


def solution(mesh):
    in_specs = (
        P("batch", None),
        P("batch", None),
        P("batch", "tower"),
        P("batch", "tower"),
        P("batch"),
    )
    out_specs = (P("batch", "tower"),) * 4
    return jax.shard_map(shards, mesh=mesh, in_specs=in_specs, out_specs=out_specs, check_vma=False)
```

```python
import functools

import jax
import jax.numpy as jnp
from jax import lax
from jax.experimental import pallas as pl
from jax.experimental.pallas import tpu as pltpu
from jax.sharding import PartitionSpec as P

sharpness = 10.0
shift = -4.0
multiplier = 262144.0
epsilon = 1e-06

F32, BF16 = jnp.float32, jnp.bfloat16


def dot(a, b, dims):
    return lax.dot_general(a, b, (dims, ((), ())), preferred_element_type=F32)


def nt(a, b):
    return dot(a, b, ((1,), (1,)))


def nn(a, b):
    return dot(a, b, ((1,), (0,)))


def up16(k):
    return -(-k // 16) * 16


def call(body, outs, scalars, arrays, us, alias=None):
    smem = pl.BlockSpec(memory_space=pltpu.SMEM)
    vmem = pl.BlockSpec(memory_space=pltpu.VMEM)
    return pl.pallas_call(
        body,
        out_shape=[jax.ShapeDtypeStruct(s, t) for s, t in outs],
        in_specs=[smem] * len(scalars) + [vmem] * len(arrays),
        out_specs=[vmem] * len(outs),
        input_output_aliases=alias or {},
        cost_estimate=pl.CostEstimate(
            flops=int(us * 2e8),
            transcendentals=0,
            bytes_accessed=sum(a.size * a.dtype.itemsize for a in arrays),
        ),
        compiler_params=pltpu.CompilerParams(vmem_limit_bytes=48 * 1024 * 1024),
    )(*scalars, *arrays)


def tie(xs):
    return lax.optimization_barrier(xs)


class Ring:
    def __init__(self, batch_size):
        n = self.n = batch_size // 2
        half = n // 2
        self.order = [2 * r if r < half else 2 * (n - 1 - r) + 1 for r in range(n)]
        self.fwd = self._perm(1)
        self.bwd = self._perm(-1)
        self.core = [(b, b ^ 1) for b in range(batch_size)]
        chip = lax.axis_index("batch") // 2
        self.pos = jnp.where(chip % 2 == 0, chip // 2, n - 1 - chip // 2)
        place = (self.pos + jnp.arange(n, dtype=jnp.int32)) % n
        self.chips = jnp.where(place < half, 2 * place, 2 * (n - 1 - place) + 1).astype(jnp.int32)

    def _perm(self, step):
        pairs = []
        for r, chip in enumerate(self.order):
            to = self.order[(r + step) % self.n]
            pairs += [(2 * chip + c, 2 * to + c) for c in range(2)]
        return pairs

    def right(self, x):
        return lax.ppermute(x, "batch", self.fwd)

    def left(self, x):
        return lax.ppermute(x, "batch", self.bwd)

    def other_core(self, x):
        return lax.ppermute(x, "batch", self.core)


def swap(x):
    return lax.ppermute(x, "tower", [(0, 1), (1, 0)])


def prepare(nb, ri, rt, rpi, rpt, core_ref, img_ref, txt_ref, ki_ref, gi_ref, kt_ref, gt_ref, *wide):
    first = core_ref[0] == 0
    rows = img_ref.shape[0]
    for feat, r, rp, keep, give in (
        (img_ref, ri, rpi, ki_ref, gi_ref),
        (txt_ref, rt, rpt, kt_ref, gt_ref),
    ):
        t = feat[...].T if r == rp else feat[...].astype(F32).T

        def block(b):
            x = t[b * r : (b + 1) * r]
            if rp > r:
                x = jnp.concatenate([x, jnp.zeros((rp - r, rows), x.dtype)])
            return x.astype(BF16)

        for q in range(nb // 2):
            a, b = block(2 * q), block(2 * q + 1)
            keep[q] = jnp.where(first, a, b)
            give[q] = jnp.where(first, b, a)
    for feat, r, rp, out in ((txt_ref, rt, rpt, wide[0]), (img_ref, ri, rpi, wide[-1])):
        if rp == r:
            out[...] = feat[...]
            continue
        out[...] = jnp.zeros_like(out)
        for b in range(nb):
            out[:, b * rp : b * rp + r] = feat[:, b * r : (b + 1) * r]


def feature_products(nb, ri, rt, s_ref, do_ref, dg_ref, wi_ref, wt_ref, keep_ref, give_ref):
    image = s_ref[0] == 0
    do, dg = do_ref[...], dg_ref[...]
    dps = jnp.where(image, do, dg), jnp.where(image, dg, do)
    h = nb // 2
    for out, tower in ((give_ref, 1 - s_ref[0]), (keep_ref, s_ref[0])):
        at = 0
        for dp, w_ref, r in ((dps[0], wi_ref, ri), (dps[1], wt_ref, rt)):
            if r == w_ref.shape[1]:
                x = nt(dp, w_ref[pl.ds(tower * h, h)].reshape(h * r, dp.shape[1]))
            else:
                x = [nt(dp, w_ref[tower * h + b])[:, :r] for b in range(h)]
                x = jnp.concatenate(x, axis=1)
            out[:, at : at + h * r] = x.astype(out.dtype)
            at += h * r


def finish(keep_ref, got_ref, img_ref, txt_ref):
    at = 0
    for out in (img_ref, txt_ref):
        cols = slice(at, at + out.shape[1])
        out[...] = (keep_ref[:, cols] + got_ref[:, cols].astype(F32)).astype(BF16)
        at += out.shape[1]


def sums(rpi, g_ref, f_ref, b_ref, img_ref, txt_ref):
    x = g_ref[...] + f_ref[...].astype(F32) + b_ref[...].astype(F32)
    img_ref[...] = x[: img_ref.shape[0]]
    txt_ref[...] = x[rpi : rpi + txt_ref.shape[0]]


def project(n, rpi, rpt, rt, half, slot_ref, img_ref, txt_ref, *refs):
    chunks, (wi_ref, wt_ref, pi_ref, pt_ref, sq_ref, count_ref) = refs[:-6], refs[-6:]
    it = iter(chunks)
    h = n // 2
    for sibling in range(2):
        for d in range(n):
            b = slot_ref[sibling, d]
            if d == h:
                wi_ref[b] = next(it)[...]
                wt_ref[b] = next(it)[...]
            else:
                c = next(it)
                wi_ref[b] = c[:rpi]
                wt_ref[b] = c[rpi:]
    count_ref[...] = jnp.broadcast_to(
        sum(wt_ref[b, :, :128].astype(F32)[rt : rt + 1] for b in range(2 * n)), (8, 128)
    )
    pi = nn(img_ref[...], wi_ref[...].reshape(2 * n * rpi, half))
    pt = nn(txt_ref[...], wt_ref[...].reshape(2 * n * rpt, half))
    pi_ref[...] = pi
    pt_ref[...] = pt
    si = jnp.sum(pi * pi, axis=1, keepdims=True)
    st = jnp.sum(pt * pt, axis=1, keepdims=True)
    lane = lax.broadcasted_iota(jnp.int32, (pi.shape[0], 128), 1)
    sq_ref[...] = jnp.where(lane == 0, si, st).T[:8]


def normalize(s_ref, pi_ref, pt_ref, sq_ref, got_ref, mine_ref, other_ref, norm_ref):
    tower, valid = s_ref[0], s_ref[1]
    rows = pi_ref.shape[0]
    sq = sq_ref[...] + got_ref[...]
    norm = jnp.sqrt(sq + epsilon).T
    ni, nt_ = norm[:, 0:1], norm[:, 1:2]
    keep = lax.broadcasted_iota(jnp.int32, (rows, 1), 0) < valid
    u = jnp.where(keep, pi_ref[...] / ni, 0.0)
    v = jnp.where(keep, pt_ref[...] / nt_, 0.0)
    image = tower == 0
    mine_ref[...] = jnp.where(image, u, v).astype(BF16)
    other_ref[...] = jnp.where(image, v, u).astype(BF16)
    norm_ref[...] = jnp.where(image, ni, nt_)


def pairs(chunks, sides, first, *refs):
    half = refs[0].shape[1]
    m = len(sides)
    mine, refs = refs[: 2 * m], refs[2 * m :]
    fs, refs = refs[: 2 * chunks], refs[2 * chunks :]
    fo = jnp.concatenate([f[...] for f in fs[:chunks]]) if chunks > 1 else fs[0][...]
    fx = jnp.concatenate([f[...] for f in fs[chunks:]]) if chunks > 1 else fs[1][...]
    ins, outs = ((), refs) if first else (refs[:m], refs[m:])
    for i, side in enumerate(sides):
        mo, mx = mine[2 * i], mine[2 * i + 1]
        s = sharpness * (nt(mo[...], fo) + nt(mx[...], fx)) + shift
        if first and side == 0:
            r = lax.broadcasted_iota(jnp.int32, s.shape, 0)
            c = lax.broadcasted_iota(jnp.int32, s.shape, 1)
            g = jax.nn.sigmoid(jnp.where(r == c, -s, s))
            g = jnp.where(r == c, -g, g)
        else:
            g = jax.nn.sigmoid(s)
        qb = g.astype(BF16)
        for at, f in ((0, fo), (half, fx)):
            part = nn(qb, f)
            cols = slice(at, at + half)
            outs[i][:, cols] = (part if first else ins[i][:, cols] + part).astype(outs[i].dtype)


def back_norm(
    s_ref, count_ref, acc_ref, got_ref, last_ref, mo_ref, mx_ref, norm_ref, do_ref, dx_ref
):
    valid = s_ref[1]
    coef = sharpness * multiplier / count_ref[0:1, 0:1]
    rows, half = mo_ref.shape
    du = (acc_ref[...] + got_ref[...] + last_ref[...].astype(F32)) * coef
    duo, dux = du[:, :half], du[:, half:]
    mo, mx = mo_ref[...].astype(F32), mx_ref[...].astype(F32)
    along = jnp.sum(mo * duo, axis=1, keepdims=True) + jnp.sum(mx * dux, axis=1, keepdims=True)
    keep = lax.broadcasted_iota(jnp.int32, (rows, 1), 0) < valid
    norm = norm_ref[...]
    do_ref[...] = jnp.where(keep, (duo - mo * along) / norm, 0.0).astype(BF16)
    dx_ref[...] = jnp.where(keep, (dux - mx * along) / norm, 0.0).astype(BF16)


def products(n, first, s_ref, chip_ref, do_ref, dg_ref, so_ref, sg_ref, ai, bi, at, bt, *outs):
    image = s_ref[0] == 0
    do, dg, so, sg = do_ref[...], dg_ref[...], so_ref[...], sg_ref[...]
    img, img_s = jnp.where(image, do, dg), jnp.where(image, so, sg)
    txt, txt_s = jnp.where(image, dg, do), jnp.where(image, sg, so)
    rpi = ai.shape[1]
    h = n // 2
    early = [h, h - 1, n - h + 1]
    for d in early if first else [d for d in range(n) if d not in early]:
        q = chip_ref[d]
        gi = nn(ai[q], img) + nn(bi[q], img_s)
        gt = nn(at[q], txt) + nn(bt[q], txt_s)
        if d == h:
            outs[0][...] = gi.astype(BF16)
            outs[1][...] = gt.astype(BF16)
        else:
            out = outs[1 + early.index(d)] if first else outs[0].at[d]
            out[:rpi] = gi
            out[rpi:] = gt


def shards(img_feat, txt_feat, img_proj, txt_proj, valid_rows):
    nb = lax.axis_size("batch")
    ring = Ring(nb)
    n, h = ring.n, ring.n // 2
    tower = lax.axis_index("tower")
    core = lax.axis_index("batch") % 2
    rows = img_feat.shape[0]
    ri, half = img_proj.shape
    rt = txt_proj.shape[0]
    rpi, rpt = up16(ri), up16(rt + 1)
    flags = jnp.stack([tower.astype(jnp.int32), valid_rows[0]])

    count_rows = jnp.broadcast_to(valid_rows.astype(BF16)[:, None], (rpt - rt, half))
    pad = jnp.zeros((rpi - ri, half), BF16)
    w = jnp.concatenate([img_proj] + [pad] * (rpi > ri) + [txt_proj, count_rows])
    prep = call(
        functools.partial(prepare, nb, ri, rt, rpi, rpt),
        [((n, rpi, rows), BF16)] * 2
        + [((n, rpt, rows), BF16)] * 2
        + [((rows, nb * rpt), BF16)]
        + [((rows, nb * rpi), BF16)],
        [core.astype(jnp.int32).reshape(1)],
        [img_feat, txt_feat],
        1,
    )
    at = {0: w}
    sib = {0: ring.other_core(w)}
    f = b = w
    for k in range(1, h):
        f, b = ring.right(f), ring.left(b)
        if k == 1:
            f, b, *prep = tie((f, b, *prep))
        at[n - k], at[k] = f, b
        sib[n - k], sib[k] = ring.other_core(f), ring.other_core(b)
    img_keep, img_give, txt_keep, txt_give, txt_wide, img_wide = prep
    f, b = ring.right(f[:rpi]), ring.left(b[rpi:])
    at[h], sib[h] = (f, b), (ring.other_core(f), ring.other_core(b))

    def flat(chunks):
        out = []
        for d in range(n):
            out += list(chunks[d]) if d == h else [chunks[d]]
        return out

    slots = jnp.stack([2 * ring.chips + core, 2 * ring.chips + 1 - core]).astype(jnp.int32)
    wi, wt, p_img, p_txt, sq, count = call(
        functools.partial(project, n, rpi, rpt, rt, half),
        [
            ((nb, rpi, half), BF16),
            ((nb, rpt, half), BF16),
            ((rows, half), F32),
            ((rows, half), F32),
            ((8, rows), F32),
            ((8, 128), F32),
        ],
        [slots],
        [img_wide, txt_wide] + flat(at) + flat(sib),
        4,
    )
    mine_o, other_o, norm = call(
        normalize,
        [((rows, half), BF16), ((rows, half), BF16), ((rows, 1), F32)],
        [flags],
        [p_img, p_txt, sq, swap(sq)],
        1,
    )

    other_x = swap(mine_o)
    other_x, late = tie((other_x, other_o))
    mine_x = swap(late)
    mine = [mine_o, mine_x, ring.other_core(mine_o), ring.other_core(mine_x)]

    def add(acc, sides, arrays, first=False, out=F32):
        chunks = len(arrays) // 2
        own = [a for side in sides for a in mine[2 * side : 2 * side + 2]]
        given = own + arrays
        return call(
            functools.partial(pairs, chunks, sides, first),
            [((rows, 2 * half), out)] * len(sides),
            [],
            given + list(acc),
            1.1 * len(sides),
            {len(given) + i: i for i in range(len(acc))},
        )

    acc = ()
    fa = ba = other_o
    fc = bc = other_x
    chunks = [[other_o, other_x]]
    cut = rows // 2
    for k in range(1, h + 1):
        if k == h:
            fa, ba, fc, bc = fa[:cut], ba[cut:], fc[:cut], bc[cut:]
        if 2 < k < h:
            acc = add(acc, (0, 1), chunks[k - 3], first=k == 3)
            fa, ba, *acc = tie((fa, ba, *acc))
        fa, ba = ring.right(fa), ring.left(ba)
        fc, bc, fa, ba = tie((fc, bc, fa, ba))
        if k > max(1, h - 2):
            acc = add(acc, (0, 1), chunks[k - 2], first=k == 2)
            fc, bc, *acc = tie((fc, bc, *acc))
        fc, bc = ring.right(fc), ring.left(bc)
        chunks.append([fa, ba, fc, bc])
    waiting = chunks[h - 1][:2] + chunks[h][:2] + chunks[h - 1][2:] + chunks[h][2:]
    got = ring.other_core(acc[1])
    (last,) = add((), (1,), waiting, first=True, out=BF16)
    last, *waiting = tie((last, *waiting))
    (mine_acc,) = add(acc[:1], (0,), waiting)
    dp_o, dp_x = call(
        back_norm,
        [((rows, half), BF16)] * 2,
        [flags],
        [count, mine_acc, got, ring.other_core(last), mine_o, mine_x, norm],
        1,
    )
    dp_got = swap(dp_x)
    dps = [dp_o, dp_got, ring.other_core(dp_o), ring.other_core(dp_got)]

    feats = [img_keep, ring.other_core(img_give), txt_keep, ring.other_core(txt_give)]

    def product(first, outs, ds):
        body = functools.partial(products, n, first)
        return call(body, outs, [flags, ring.chips], ds + feats, 1 if first else 2)

    chunk = ((rpi + rpt, half), F32)
    f, b, gf, gb = product(True, [((rpi, half), BF16), ((rpt, half), BF16), chunk, chunk], dps)
    dp_o, dp_got, f, b = tie((dp_o, dp_got, f, b))
    keep, give = call(
        functools.partial(feature_products, nb, ri, rt),
        [((rows, nb * (ri + rt) // 2), F32), ((rows, nb * (ri + rt) // 2), BF16)],
        [flags],
        [dp_o, dp_got, wi, wt],
        3,
    )

    f, b = ring.right(f), ring.left(b)
    f, *late = tie((f, *dps))
    (g,) = product(False, [((n, rpi + rpt, half), F32)], late)
    for k in range(h - 1, 0, -1):
        pf, pb = (gf, gb) if k == h - 1 else (g[k], g[n - k])
        if k == h - 1:
            f = jnp.concatenate([pf[:rpi] + f.astype(F32), pf[rpi:]])
            b = jnp.concatenate([pb[:rpi], pb[rpi:] + b.astype(F32)])
        else:
            f, b = pf + f.astype(F32), pb + b.astype(F32)
        f, b = f.astype(BF16), b.astype(BF16)
        if k == h - 2:
            f, b, keep, give = tie((f, b, keep, give))
        f, b = ring.right(f), ring.left(b)
    got = swap(give)
    img_grad, txt_grad = call(
        finish,
        [((rows, nb * r // 2), BF16) for r in (ri, rt)],
        [],
        [keep, got],
        10,
    )
    f, b, img_grad, txt_grad = tie((f, b, img_grad, txt_grad))
    img_total, txt_total = call(
        functools.partial(sums, rpi),
        [((ri, half), F32), ((rt, half), F32)],
        [],
        [g[0], f, b],
        1,
    )
    return img_grad, txt_grad, img_total, txt_total


def solution(mesh):
    in_specs = (
        P("batch", None),
        P("batch", None),
        P("batch", "tower"),
        P("batch", "tower"),
        P("batch"),
    )
    out_specs = (P("batch", "tower"),) * 4
    return jax.shard_map(shards, mesh=mesh, in_specs=in_specs, out_specs=out_specs, check_vma=False)
```

```python
import functools

import jax
import jax.numpy as jnp
from jax import lax
from jax.experimental import pallas as pl
from jax.experimental.pallas import tpu as pltpu
from jax.sharding import PartitionSpec as P

sharpness = 10.0
shift = -4.0
multiplier = 262144.0
epsilon = 1e-06

F32, BF16 = jnp.float32, jnp.bfloat16


def dot(a, b, dims):
    return lax.dot_general(a, b, (dims, ((), ())), preferred_element_type=F32)


def nt(a, b):
    return dot(a, b, ((1,), (1,)))


def nn(a, b):
    return dot(a, b, ((1,), (0,)))


def up16(k):
    return -(-k // 16) * 16


def call(body, outs, scalars, arrays, us, alias=None):
    smem = pl.BlockSpec(memory_space=pltpu.SMEM)
    vmem = pl.BlockSpec(memory_space=pltpu.VMEM)
    return pl.pallas_call(
        body,
        out_shape=[jax.ShapeDtypeStruct(s, t) for s, t in outs],
        in_specs=[smem] * len(scalars) + [vmem] * len(arrays),
        out_specs=[vmem] * len(outs),
        input_output_aliases=alias or {},
        cost_estimate=pl.CostEstimate(
            flops=int(us * 2e8),
            transcendentals=0,
            bytes_accessed=sum(a.size * a.dtype.itemsize for a in arrays),
        ),
        compiler_params=pltpu.CompilerParams(vmem_limit_bytes=48 * 1024 * 1024),
    )(*scalars, *arrays)


def tie(xs):
    return lax.optimization_barrier(xs)


class Ring:
    def __init__(self, batch_size):
        n = self.n = batch_size // 2
        half = n // 2
        self.order = [2 * r if r < half else 2 * (n - 1 - r) + 1 for r in range(n)]
        self.fwd = self._perm(1)
        self.bwd = self._perm(-1)
        self.core = [(b, b ^ 1) for b in range(batch_size)]
        chip = lax.axis_index("batch") // 2
        self.pos = jnp.where(chip % 2 == 0, chip // 2, n - 1 - chip // 2)
        place = (self.pos + jnp.arange(n, dtype=jnp.int32)) % n
        self.chips = jnp.where(place < half, 2 * place, 2 * (n - 1 - place) + 1).astype(jnp.int32)

    def _perm(self, step):
        pairs = []
        for r, chip in enumerate(self.order):
            to = self.order[(r + step) % self.n]
            pairs += [(2 * chip + c, 2 * to + c) for c in range(2)]
        return pairs

    def right(self, x):
        return lax.ppermute(x, "batch", self.fwd)

    def left(self, x):
        return lax.ppermute(x, "batch", self.bwd)

    def other_core(self, x):
        return lax.ppermute(x, "batch", self.core)


def swap(x):
    return lax.ppermute(x, "tower", [(0, 1), (1, 0)])


def prepare(nb, ri, rt, rpi, rpt, core_ref, img_ref, txt_ref, ki_ref, gi_ref, kt_ref, gt_ref, *wide):
    first = core_ref[0] == 0
    rows = img_ref.shape[0]
    for feat, r, rp, keep, give in (
        (img_ref, ri, rpi, ki_ref, gi_ref),
        (txt_ref, rt, rpt, kt_ref, gt_ref),
    ):
        t = feat[...].T if r == rp else feat[...].astype(F32).T

        def block(b):
            x = t[b * r : (b + 1) * r]
            if rp > r:
                x = jnp.concatenate([x, jnp.zeros((rp - r, rows), x.dtype)])
            return x.astype(BF16)

        for q in range(nb // 2):
            a, b = block(2 * q), block(2 * q + 1)
            keep[q] = jnp.where(first, a, b)
            give[q] = jnp.where(first, b, a)
    for feat, r, rp, out in ((txt_ref, rt, rpt, wide[0]), (img_ref, ri, rpi, wide[-1])):
        if rp == r:
            out[...] = feat[...]
            continue
        out[...] = jnp.zeros_like(out)
        for b in range(nb):
            out[:, b * rp : b * rp + r] = feat[:, b * r : (b + 1) * r]


def feature_products(nb, ri, rt, own, s_ref, do_ref, dg_ref, wi_ref, wt_ref, out_ref):
    image = s_ref[0] == 0
    do, dg = do_ref[...], dg_ref[...]
    dps = jnp.where(image, do, dg), jnp.where(image, dg, do)
    h = nb // 2
    base = (s_ref[0] if own else 1 - s_ref[0]) * h
    at = 0
    for dp, w_ref, r in ((dps[0], wi_ref, ri), (dps[1], wt_ref, rt)):
        if r == w_ref.shape[1]:
            x = nt(dp, w_ref[pl.ds(base, h)].reshape(h * r, dp.shape[1]))
        else:
            x = jnp.concatenate([nt(dp, w_ref[base + b])[:, :r] for b in range(h)], axis=1)
        out_ref[:, at : at + h * r] = x.astype(out_ref.dtype)
        at += h * r


def finish(keep_ref, got_ref, img_ref, txt_ref):
    at = 0
    for out in (img_ref, txt_ref):
        cols = slice(at, at + out.shape[1])
        out[...] = (keep_ref[:, cols] + got_ref[:, cols].astype(F32)).astype(BF16)
        at += out.shape[1]


def sums(rpi, g_ref, f_ref, b_ref, img_ref, txt_ref):
    x = g_ref[...] + f_ref[...].astype(F32) + b_ref[...].astype(F32)
    img_ref[...] = x[: img_ref.shape[0]]
    txt_ref[...] = x[rpi : rpi + txt_ref.shape[0]]


def project(n, rpi, rpt, rt, half, slot_ref, img_ref, txt_ref, *refs):
    chunks, (wi_ref, wt_ref, pi_ref, pt_ref, sq_ref, count_ref) = refs[:-6], refs[-6:]
    it = iter(chunks)
    h = n // 2
    for sibling in range(2):
        for d in range(n):
            b = slot_ref[sibling, d]
            if d == h:
                wi_ref[b] = next(it)[...]
                wt_ref[b] = next(it)[...]
            else:
                c = next(it)
                wi_ref[b] = c[:rpi]
                wt_ref[b] = c[rpi:]
    count_ref[...] = jnp.broadcast_to(
        sum(wt_ref[b, :, :128].astype(F32)[rt : rt + 1] for b in range(2 * n)), (8, 128)
    )
    pi = nn(img_ref[...], wi_ref[...].reshape(2 * n * rpi, half))
    pt = nn(txt_ref[...], wt_ref[...].reshape(2 * n * rpt, half))
    pi_ref[...] = pi
    pt_ref[...] = pt
    si = jnp.sum(pi * pi, axis=1, keepdims=True)
    st = jnp.sum(pt * pt, axis=1, keepdims=True)
    lane = lax.broadcasted_iota(jnp.int32, (pi.shape[0], 128), 1)
    sq_ref[...] = jnp.where(lane == 0, si, st).T[:8]


def normalize(s_ref, pi_ref, pt_ref, sq_ref, got_ref, mine_ref, other_ref, norm_ref):
    tower, valid = s_ref[0], s_ref[1]
    rows = pi_ref.shape[0]
    sq = sq_ref[...] + got_ref[...]
    norm = jnp.sqrt(sq + epsilon).T
    ni, nt_ = norm[:, 0:1], norm[:, 1:2]
    keep = lax.broadcasted_iota(jnp.int32, (rows, 1), 0) < valid
    u = jnp.where(keep, pi_ref[...] / ni, 0.0)
    v = jnp.where(keep, pt_ref[...] / nt_, 0.0)
    image = tower == 0
    mine_ref[...] = jnp.where(image, u, v).astype(BF16)
    other_ref[...] = jnp.where(image, v, u).astype(BF16)
    norm_ref[...] = jnp.where(image, ni, nt_)


def pairs(chunks, sides, first, *refs):
    half = refs[0].shape[1]
    m = len(sides)
    mine, refs = refs[: 2 * m], refs[2 * m :]
    fs, refs = refs[: 2 * chunks], refs[2 * chunks :]
    fo = jnp.concatenate([f[...] for f in fs[:chunks]]) if chunks > 1 else fs[0][...]
    fx = jnp.concatenate([f[...] for f in fs[chunks:]]) if chunks > 1 else fs[1][...]
    ins, outs = ((), refs) if first else (refs[:m], refs[m:])
    for i, side in enumerate(sides):
        mo, mx = mine[2 * i], mine[2 * i + 1]
        s = sharpness * (nt(mo[...], fo) + nt(mx[...], fx)) + shift
        if first and side == 0:
            r = lax.broadcasted_iota(jnp.int32, s.shape, 0)
            c = lax.broadcasted_iota(jnp.int32, s.shape, 1)
            g = jax.nn.sigmoid(jnp.where(r == c, -s, s))
            g = jnp.where(r == c, -g, g)
        else:
            g = jax.nn.sigmoid(s)
        qb = g.astype(BF16)
        for at, f in ((0, fo), (half, fx)):
            part = nn(qb, f)
            cols = slice(at, at + half)
            outs[i][:, cols] = (part if first else ins[i][:, cols] + part).astype(outs[i].dtype)


def back_norm(
    s_ref, count_ref, acc_ref, got_ref, last_ref, mo_ref, mx_ref, norm_ref, do_ref, dx_ref
):
    valid = s_ref[1]
    coef = sharpness * multiplier / count_ref[0:1, 0:1]
    rows, half = mo_ref.shape
    du = (acc_ref[...] + got_ref[...] + last_ref[...].astype(F32)) * coef
    duo, dux = du[:, :half], du[:, half:]
    mo, mx = mo_ref[...].astype(F32), mx_ref[...].astype(F32)
    along = jnp.sum(mo * duo, axis=1, keepdims=True) + jnp.sum(mx * dux, axis=1, keepdims=True)
    keep = lax.broadcasted_iota(jnp.int32, (rows, 1), 0) < valid
    norm = norm_ref[...]
    do_ref[...] = jnp.where(keep, (duo - mo * along) / norm, 0.0).astype(BF16)
    dx_ref[...] = jnp.where(keep, (dux - mx * along) / norm, 0.0).astype(BF16)


def products(n, first, s_ref, chip_ref, do_ref, dg_ref, so_ref, sg_ref, ai, bi, at, bt, *outs):
    image = s_ref[0] == 0
    do, dg, so, sg = do_ref[...], dg_ref[...], so_ref[...], sg_ref[...]
    img, img_s = jnp.where(image, do, dg), jnp.where(image, so, sg)
    txt, txt_s = jnp.where(image, dg, do), jnp.where(image, sg, so)
    rpi = ai.shape[1]
    h = n // 2
    early = [h, h - 1, n - h + 1]
    for d in early if first else [d for d in range(n) if d not in early]:
        q = chip_ref[d]
        gi = nn(ai[q], img) + nn(bi[q], img_s)
        gt = nn(at[q], txt) + nn(bt[q], txt_s)
        if d == h:
            outs[0][...] = gi.astype(BF16)
            outs[1][...] = gt.astype(BF16)
        else:
            out = outs[1 + early.index(d)] if first else outs[0].at[d]
            out[:rpi] = gi
            out[rpi:] = gt


def shards(img_feat, txt_feat, img_proj, txt_proj, valid_rows):
    nb = lax.axis_size("batch")
    ring = Ring(nb)
    n, h = ring.n, ring.n // 2
    tower = lax.axis_index("tower")
    core = lax.axis_index("batch") % 2
    rows = img_feat.shape[0]
    ri, half = img_proj.shape
    rt = txt_proj.shape[0]
    rpi, rpt = up16(ri), up16(rt + 1)
    flags = jnp.stack([tower.astype(jnp.int32), valid_rows[0]])

    count_rows = jnp.broadcast_to(valid_rows.astype(BF16)[:, None], (rpt - rt, half))
    pad = jnp.zeros((rpi - ri, half), BF16)
    w = jnp.concatenate([img_proj] + [pad] * (rpi > ri) + [txt_proj, count_rows])
    prep = call(
        functools.partial(prepare, nb, ri, rt, rpi, rpt),
        [((n, rpi, rows), BF16)] * 2
        + [((n, rpt, rows), BF16)] * 2
        + [((rows, nb * rpt), BF16)]
        + [((rows, nb * rpi), BF16)],
        [core.astype(jnp.int32).reshape(1)],
        [img_feat, txt_feat],
        1,
    )
    at = {0: w}
    sib = {0: ring.other_core(w)}
    f = b = w
    for k in range(1, h):
        f, b = ring.right(f), ring.left(b)
        if k == 1:
            f, b, *prep = tie((f, b, *prep))
        at[n - k], at[k] = f, b
        sib[n - k], sib[k] = ring.other_core(f), ring.other_core(b)
    img_keep, img_give, txt_keep, txt_give, txt_wide, img_wide = prep
    f, b = ring.right(f[:rpi]), ring.left(b[rpi:])
    at[h], sib[h] = (f, b), (ring.other_core(f), ring.other_core(b))

    def flat(chunks):
        out = []
        for d in range(n):
            out += list(chunks[d]) if d == h else [chunks[d]]
        return out

    slots = jnp.stack([2 * ring.chips + core, 2 * ring.chips + 1 - core]).astype(jnp.int32)
    wi, wt, p_img, p_txt, sq, count = call(
        functools.partial(project, n, rpi, rpt, rt, half),
        [
            ((nb, rpi, half), BF16),
            ((nb, rpt, half), BF16),
            ((rows, half), F32),
            ((rows, half), F32),
            ((8, rows), F32),
            ((8, 128), F32),
        ],
        [slots],
        [img_wide, txt_wide] + flat(at) + flat(sib),
        4,
    )
    mine_o, other_o, norm = call(
        normalize,
        [((rows, half), BF16), ((rows, half), BF16), ((rows, 1), F32)],
        [flags],
        [p_img, p_txt, sq, swap(sq)],
        1,
    )

    other_x = swap(mine_o)
    other_x, late = tie((other_x, other_o))
    mine_x = swap(late)
    mine = [mine_o, mine_x, ring.other_core(mine_o), ring.other_core(mine_x)]

    def add(acc, sides, arrays, first=False, out=F32):
        chunks = len(arrays) // 2
        own = [a for side in sides for a in mine[2 * side : 2 * side + 2]]
        given = own + arrays
        return call(
            functools.partial(pairs, chunks, sides, first),
            [((rows, 2 * half), out)] * len(sides),
            [],
            given + list(acc),
            1.1 * len(sides),
            {len(given) + i: i for i in range(len(acc))},
        )

    acc = ()
    fa = ba = other_o
    fc = bc = other_x
    chunks = [[other_o, other_x]]
    cut = rows // 2
    for k in range(1, h + 1):
        if k == h:
            fa, ba, fc, bc = fa[:cut], ba[cut:], fc[:cut], bc[cut:]
        if 2 < k < h:
            acc = add(acc, (0, 1), chunks[k - 3], first=k == 3)
            fa, ba, *acc = tie((fa, ba, *acc))
        fa, ba = ring.right(fa), ring.left(ba)
        fc, bc, fa, ba = tie((fc, bc, fa, ba))
        if k > max(1, h - 2):
            acc = add(acc, (0, 1), chunks[k - 2], first=k == 2)
            fc, bc, *acc = tie((fc, bc, *acc))
        fc, bc = ring.right(fc), ring.left(bc)
        chunks.append([fa, ba, fc, bc])
    waiting = chunks[h - 1][:2] + chunks[h][:2] + chunks[h - 1][2:] + chunks[h][2:]
    got = ring.other_core(acc[1])
    (last,) = add((), (1,), waiting, first=True, out=BF16)
    last, *waiting = tie((last, *waiting))
    (mine_acc,) = add(acc[:1], (0,), waiting)
    dp_o, dp_x = call(
        back_norm,
        [((rows, half), BF16)] * 2,
        [flags],
        [count, mine_acc, got, ring.other_core(last), mine_o, mine_x, norm],
        1,
    )
    dp_got = swap(dp_x)
    dps = [dp_o, dp_got, ring.other_core(dp_o), ring.other_core(dp_got)]

    feats = [img_keep, ring.other_core(img_give), txt_keep, ring.other_core(txt_give)]

    def product(first, outs, ds):
        body = functools.partial(products, n, first)
        return call(body, outs, [flags, ring.chips], ds + feats, 1 if first else 2)

    chunk = ((rpi + rpt, half), F32)
    f, b, gf, gb = product(True, [((rpi, half), BF16), ((rpt, half), BF16), chunk, chunk], dps)
    dp_o, dp_got, f, b = tie((dp_o, dp_got, f, b))
    def feature_part(own, kind):
        return call(
            functools.partial(feature_products, nb, ri, rt, own),
            [((rows, nb * (ri + rt) // 2), kind)],
            [flags],
            [dp_o, dp_got, wi, wt],
            2,
        )[0]

    keep, give = feature_part(True, F32), feature_part(False, BF16)
    f, b = ring.right(f), ring.left(b)
    f, _, *late = tie((f, give, *dps))
    (g,) = product(False, [((n, rpi + rpt, half), F32)], late)
    for k in range(h - 1, 0, -1):
        pf, pb = (gf, gb) if k == h - 1 else (g[k], g[n - k])
        if k == h - 1:
            f = jnp.concatenate([pf[:rpi] + f.astype(F32), pf[rpi:]])
            b = jnp.concatenate([pb[:rpi], pb[rpi:] + b.astype(F32)])
        else:
            f, b = pf + f.astype(F32), pb + b.astype(F32)
        f, b = f.astype(BF16), b.astype(BF16)
        if k == h - 2:
            f, b = tie((f, b))
        if k == 1:
            f, b, keep = tie((f, b, keep))
        f, b = ring.right(f), ring.left(b)
    got = swap(give)
    img_grad, txt_grad = call(
        finish,
        [((rows, nb * r // 2), BF16) for r in (ri, rt)],
        [],
        [keep, got],
        10,
    )
    f, b, img_grad, txt_grad = tie((f, b, img_grad, txt_grad))
    img_total, txt_total = call(
        functools.partial(sums, rpi),
        [((ri, half), F32), ((rt, half), F32)],
        [],
        [g[0], f, b],
        1,
    )
    return img_grad, txt_grad, img_total, txt_total


def solution(mesh):
    in_specs = (
        P("batch", None),
        P("batch", None),
        P("batch", "tower"),
        P("batch", "tower"),
        P("batch"),
    )
    out_specs = (P("batch", "tower"),) * 4
    return jax.shard_map(shards, mesh=mesh, in_specs=in_specs, out_specs=out_specs, check_vma=False)
```
